512 devices in a mesh: member: 32 (over z_hi, x, y), domain: 16 (over z_lo, core).
Axes of the slice: x: 4, y: 4, z: 16 (z_hi: 2, z_lo: 8; z = z_hi * 8 + z_lo), core: 2. Of those that a mesh axis runs over, the one named last changes fastest.
Arguments:
- ensemble: bfloat16 [1024, 2, 64, 2048], P('member', None, None, 'domain'), may hold values from -4 to 4
- obs_value: float32 [32, 4096], P('member', 'domain'), may hold values from -6 to 6
- obs_prec: float32 [32, 4096], P('member', 'domain'), may hold values from 1 to 10
- obs_row: int32 [32, 4096], P('member', 'domain'), may hold values from 0 to 1
- obs_col: int32 [32, 4096], P('member', 'domain'), may hold values from 0 to 127
- loc_mask: int32 [32, 64], P('member', 'domain'), may hold values 0 or 1
Outputs:
- analysis: bfloat16 [1024, 2, 64, 2048], P('member', None, None, 'domain')
The draws below stay inside these ranges and needn't reach their ends.
All inputs are finite; a program needn't handle non-finite values. No bound on the sum of `loc_mask` on one device may be relied on, other than what follows from the above.
Results may differ from the reference program's by a relative error of at most 0.0075.
Values may be sent and summed in bfloat16 or wider, within the bound.
No kernel may reach another device: no remote copies, remote signals or barrier semaphores. Data moves between devices by JAX's collectives and lax.ppermute only.
A program may use at most 64 MiB of HBM per device.

```python
import math
import jax
import jax.numpy as jnp
from jax import lax

MEMBERS = 1024
REGION_ROWS = 2
REGION_COLUMNS = 128
P_OWN = 256
ROWS = 64
COLS = 2048
OBS_COLS = 4096
MASK_COLS = 64
N_MEMBER = 32
N_DOMAIN = 16


def plant(entries, stream_key, smallest, top_value):
    longest = entries.shape.index(max(entries.shape))
    spots = []
    for shift in (0, 1):
        where = [jax.random.randint(jax.random.fold_in(stream_key, axis), (), 0, length) for axis, length in enumerate(entries.shape)]
        where[longest] = (where[longest] + shift) % entries.shape[longest]
        spots.append(tuple(where))
    return entries.at[spots[0]].set(smallest).at[spots[1]].set(top_value)


def level_of(stream_key, dims, shards, smallest, high):
    factor_of = 1.0
    for dim, blocks in shards:
        draws = jax.random.uniform(jax.random.fold_in(jax.random.fold_in(stream_key, 6), dim), (blocks,), jnp.float32, smallest / len(shards), high / len(shards))
        factor_of = factor_of * jnp.repeat(jnp.exp(draws), dims[dim] // blocks).reshape((-1,) + (1,) * (len(dims) - 1 - dim))
    return factor_of


def bell_draw(own_key, dims, spread, most, pieces=(), kind=jnp.bfloat16):
    loudness = level_of(own_key, dims, pieces, -0.22, 0.18) if pieces else 1.0
    entries = jax.random.normal(own_key, dims, jnp.float32) * spread * loudness
    return jnp.minimum(jnp.maximum(entries, -most), most).astype(kind)


def setup_inputs(seed: int = 0) -> dict:
    key_list = jax.random.split(jax.random.key(seed), 7)
    ensemble = bell_draw(key_list[0], (MEMBERS, 2, ROWS, COLS), 1.0, 4.0, ((0, 32), (3, 16)))
    obs_value = bell_draw(key_list[1], (N_MEMBER, OBS_COLS), 1.0, 6.0, ((0, 32), (1, 16)), jnp.float32)
    obs_prec = jnp.clip(jnp.exp(math.log(10.0) - 2.3025851 * jax.random.uniform(key_list[2], (N_MEMBER, OBS_COLS), jnp.float32) ** level_of(key_list[2], (N_MEMBER, OBS_COLS), ((0, 32), (1, 16)), -0.2, 0.2)), 1.0, 10.0)
    obs_row = plant(jax.random.randint(key_list[3], (N_MEMBER, OBS_COLS), 0, REGION_ROWS), jax.random.fold_in(key_list[3], 1), 0, REGION_ROWS - 1).astype(jnp.int32)
    obs_col = plant(jax.random.randint(key_list[4], (N_MEMBER, OBS_COLS), 0, REGION_COLUMNS), jax.random.fold_in(key_list[4], 1), 0, REGION_COLUMNS - 1).astype(jnp.int32)
    loc_mask = plant((jax.random.randint(key_list[5], (N_MEMBER, MASK_COLS), 0, 4) < 3).astype(jnp.int32), jax.random.fold_in(key_list[5], 1), 0, 1)
    return {"ensemble": ensemble, "obs_value": obs_value, "obs_prec": obs_prec, "obs_row": obs_row, "obs_col": obs_col, "loc_mask": loc_mask}


ADVECT = 0.4
DIFFUSE = 0.15
OBS_WIND = 0.5

def step_forward(central_cell, east_cells, west_cells, north_cells, south_cells):
    middle = central_cell.astype(jnp.float32)
    east_side = east_cells.astype(jnp.float32)
    west_side = west_cells.astype(jnp.float32)
    laplace = east_side + west_side + north_cells.astype(jnp.float32) + south_cells.astype(jnp.float32) - 4.0 * middle
    wind_field = middle[:, 0:1]
    return (middle - ADVECT * 0.5 * wind_field * (east_side - west_side) + DIFFUSE * laplace).astype(jnp.bfloat16)

def observe(local_region, obs_index, observed, precision):
    member_states = local_region.shape[0]
    wind_field = local_region[:, 0].reshape(member_states, -1)
    tracer = local_region[:, 1].reshape(member_states, -1)
    equivalent = jnp.take(tracer, obs_index, axis=1).astype(jnp.float32) + OBS_WIND * jnp.take(wind_field, obs_index, axis=1).astype(jnp.float32)
    central_cell = lax.optimization_barrier(jnp.mean(equivalent, axis=0))
    scaled = (equivalent - central_cell) * (member_states - 1) ** (-0.5)
    return jnp.concatenate([scaled, (observed - central_cell)[None], precision[None]], axis=0).astype(jnp.bfloat16)

def block_weights(local_rows, block_mask, parts):
    member_states = local_rows.shape[0] - 2
    tapering = jnp.array([0.5, 1.0, 1.0, 0.5], jnp.float32) * block_mask.astype(jnp.float32)
    block_cols = local_rows.shape[1] // len(parts)
    factor = jnp.repeat(tapering[jnp.array(parts)], block_cols)
    return local_rows[member_states + 1].astype(jnp.float32) * factor

def contributions(local_rows, weight):
    member_states = local_rows.shape[0] - 2
    anomaly_obs = local_rows[:member_states]
    innovation = local_rows[member_states].astype(jnp.float32)
    weighted = (anomaly_obs.astype(jnp.float32) * weight).astype(jnp.bfloat16)
    cross_term = lax.dot_general(weighted, anomaly_obs, (((1,), (1,)), ((), ())), preferred_element_type=jnp.float32)
    forcing = jnp.dot(weighted.astype(jnp.float32), innovation, precision=lax.Precision.HIGHEST)
    return (cross_term, forcing)

def analyse(local_region, cross_term, forcing):
    member_states = local_region.shape[0]
    cells = local_region.reshape(member_states, -1)
    ens_mean = lax.optimization_barrier(jnp.mean(cells.astype(jnp.float32), axis=0))
    anomalies = (cells.astype(jnp.float32) - ens_mean).astype(jnp.bfloat16)
    identity = jnp.eye(member_states, dtype=jnp.float32)
    cross_half = cross_term.astype(jnp.bfloat16)
    squared = jnp.dot(cross_half, cross_half, preferred_element_type=jnp.float32)
    row_bound = jnp.sqrt(jnp.max(lax.optimization_barrier(jnp.sum(jnp.abs(squared), axis=1))))
    half_width = (row_bound + 1.0) / 2.0
    theta = 1.0 + half_width
    ratio_sigma = theta / half_width
    rho_first = 1.0 / ratio_sigma
    first_resid = (1.0 - 1.0 / theta) * identity - cross_term / theta
    first_step = first_resid / theta
    applied = first_step + ((theta - 1.0) * cross_term - squared) / (theta * theta)
    second_resid = first_resid - applied
    rho_second = 1.0 / (2.0 * ratio_sigma - rho_first)
    second_step = rho_second * rho_first * first_step + 2.0 * rho_second / half_width * second_resid
    inverse = identity / theta + first_step + second_step
    mean_weights = jnp.dot(inverse, forcing, precision=lax.Precision.HIGHEST)
    transform = (0.5 * (identity + inverse) + mean_weights[:, None] * (member_states - 1) ** (-0.5)).astype(jnp.bfloat16)
    increment = lax.dot_general(transform, anomalies, (((0,), (0,)), ((), ())), preferred_element_type=jnp.float32)
    return (ens_mean + increment).astype(jnp.bfloat16).reshape(local_region.shape)

def reference(ensemble, obs_value, obs_prec, obs_row, obs_col, loc_mask):
    member_states = ensemble.shape[0]
    padded_region = jnp.concatenate([ensemble[..., -1:], ensemble, ensemble[..., :1]], axis=3)
    central_cell = padded_region[..., 1:-1]
    predicted_state = step_forward(central_cell, padded_region[..., 2:], padded_region[..., :-2], jnp.roll(central_cell, -1, axis=2), jnp.roll(central_cell, 1, axis=2))
    fixed_point = jnp.zeros((), jnp.int32)
    count = N_MEMBER * N_DOMAIN
    half_cols = P_OWN // 2

    def region_of(region_id):
        row_strip = (region_id // N_DOMAIN).astype(jnp.int32)
        column_block = (region_id % N_DOMAIN).astype(jnp.int32)
        local_region = lax.dynamic_slice(predicted_state, (fixed_point, fixed_point, row_strip * REGION_ROWS, column_block * REGION_COLUMNS), (member_states, 2, REGION_ROWS, REGION_COLUMNS))
        return (local_region, row_strip, column_block)

    def make_rows(region_id):
        local_region, row_strip, column_block = region_of(region_id)
        start = column_block * P_OWN
        observed = lax.dynamic_slice(obs_value, (row_strip, start), (1, P_OWN))[0]
        precision = lax.dynamic_slice(obs_prec, (row_strip, start), (1, P_OWN))[0]
        rows_at = lax.dynamic_slice(obs_row, (row_strip, start), (1, P_OWN))[0]
        cols_at = lax.dynamic_slice(obs_col, (row_strip, start), (1, P_OWN))[0]
        return observe(local_region, rows_at * REGION_COLUMNS + cols_at, observed, precision)
    stacked = lax.map(make_rows, jnp.arange(count, dtype=jnp.int32))

    def make_analysis(region_id):
        local_region, row_strip, column_block = region_of(region_id)
        left_id = row_strip * N_DOMAIN + (column_block + N_DOMAIN - 1) % N_DOMAIN
        right_id = row_strip * N_DOMAIN + (column_block + 1) % N_DOMAIN
        local_rows = jnp.concatenate([stacked[left_id][:, half_cols:], stacked[region_id], stacked[right_id][:, :half_cols]], axis=1)
        block_mask = lax.dynamic_slice(loc_mask, (row_strip, column_block * 4), (1, 4))[0]
        weight = block_weights(local_rows, block_mask, [0, 1, 2, 3])
        cross_term, forcing = contributions(local_rows, weight)
        return analyse(local_region, cross_term, forcing)
    results = lax.map(make_analysis, jnp.arange(count, dtype=jnp.int32))
    results = results.reshape(N_MEMBER, N_DOMAIN, member_states, 2, REGION_ROWS, REGION_COLUMNS)
    results = jnp.transpose(results, (2, 3, 0, 4, 1, 5))
    return results.reshape(member_states, 2, REGION_ROWS * N_MEMBER, REGION_COLUMNS * N_DOMAIN)
```

```python
import jax
import jax.numpy as jnp
from jax import lax
from jax.experimental import pallas as pl
from jax.experimental.pallas import tpu as pltpu
from jax.sharding import PartitionSpec as P

ADVECT = 0.4
DIFFUSE = 0.15
OBS_WIND = 0.5
F32 = jnp.float32
BF16 = jnp.bfloat16
VMEM = pl.BlockSpec(memory_space=pltpu.VMEM)
SMEM = pl.BlockSpec(memory_space=pltpu.SMEM)
PARAMS = pltpu.CompilerParams(vmem_limit_bytes=40 * 1024 * 1024)


def call(kernel, shapes, args, scratch=(), specs=None, flops=0):
    nbytes = sum(a.size * a.dtype.itemsize for a in args)
    return pl.pallas_call(
        kernel,
        out_shape=shapes,
        in_specs=specs or [VMEM] * len(args),
        out_specs=jax.tree.map(lambda _: VMEM, shapes),
        scratch_shapes=list(scratch),
        compiler_params=PARAMS,
        cost_estimate=pl.CostEstimate(flops=flops, bytes_accessed=nbytes, transcendentals=0),
    )(*args)


def iota(shape, dim):
    return lax.broadcasted_iota(jnp.int32, shape, dim)


def to_col(row):
    n = row.shape[1]
    return jnp.sum(jnp.where(iota((n, n), 0) == iota((n, n), 1), row, 0.0), axis=1, keepdims=True)


def to_row(col):
    n = col.shape[0]
    return jnp.sum(jnp.where(iota((n, n), 0) == iota((n, n), 1), col, 0.0), axis=0, keepdims=True)


def edge_kernel(ens_ref, head_ref, tail_ref):
    pick = jnp.where(
        (iota((8, 128), 0) == 0) & (iota((8, 128), 1) == 0)
        | (iota((8, 128), 0) == 1) & (iota((8, 128), 1) == 127),
        1.0,
        0.0,
    ).astype(BF16)
    members = ens_ref.shape[0] // 8
    for k in range(8):
        rows = ens_ref[k * members : (k + 1) * members].reshape(-1, 128)
        edges = lax.dot_general(pick, rows, (((1,), (1,)), ((), ())), preferred_element_type=F32)
        head_ref[k : k + 1, :] = edges[0:1]
        tail_ref[k : k + 1, :] = edges[1:2]


def forecast_kernel(ens_ref, west_ref, east_ref, out_ref, store):
    members, _, rows, cols = ens_ref.shape
    group = members // 8
    spot = iota((8, cols), 0)
    lane8 = iota((8, cols), 1)
    pick = jnp.where((spot == 0) & (lane8 == 0) | (spot == 1) & (lane8 == cols - 1), 1.0, 0.0).astype(BF16)

    for k in range(8):
        n = group * 2 * rows
        which = iota((8, n), 0)
        edges = jnp.where(which == 0, west_ref[k : k + 1, :], jnp.where(which == 1, east_ref[k : k + 1, :], 0.0))
        rim = lax.dot_general(
            edges.astype(BF16), pick, (((0,), (0,)), ((), ())), preferred_element_type=F32
        ).reshape(group * 2, rows, cols)
        for i in range(group):
            m = k * group + i
            wind = None
            for f in range(2):
                x = ens_ref[m, f].astype(F32)
                edge = rim[i * 2 + f]
                lane = iota((rows, cols), 1)
                east = jnp.where(lane == cols - 1, edge, pltpu.roll(x, cols - 1, 1))
                west = jnp.where(lane == 0, edge, pltpu.roll(x, 1, 1))
                north = pltpu.roll(x, rows - 1, 0)
                south = pltpu.roll(x, 1, 0)
                if f == 0:
                    wind = x
                laplace = east + west + north + south - 4.0 * x
                new = x - ADVECT * 0.5 * wind * (east - west) + DIFFUSE * laplace
                store[f, m * rows : (m + 1) * rows, :] = new
    for f in range(2):
        for r in range(rows):
            part = store[f, pl.ds(r, members, stride=rows), :]
            at = (f * 2 + r % 2) * cols
            out_ref[r // 2, :, at : at + cols] = part.astype(BF16)


def restore_kernel(in_ref, out_ref, store):
    members, _, rows, cols = out_ref.shape
    for f in range(2):
        for r in range(rows):
            at = (f * 2 + r % 2) * cols
            store[f, pl.ds(r, members, stride=rows), :] = in_ref[r // 2, :, at : at + cols].astype(F32)
    for f in range(2):
        for m in range(members):
            out_ref[m, f] = store[f, m * rows : (m + 1) * rows, :].astype(BF16)


def observe_kernel(local_ref, index_ref, value_ref, prec_ref, y_ref, head_ref, tail_ref):
    members, cells = local_ref.shape
    half = cells // 2
    equivalent = local_ref[:, half:].astype(F32) + OBS_WIND * local_ref[:, :half].astype(F32)
    mean = jnp.sum(equivalent, axis=0, keepdims=True) * (1.0 / members)
    y = ((equivalent - mean) * (members - 1) ** (-0.5)).astype(BF16)
    y_ref[...] = y
    n = index_ref.shape[1]
    hit = iota((half, n), 0) == index_ref[...]
    rows = jnp.dot(y, hit.astype(BF16), preferred_element_type=F32).astype(BF16)
    observed_mean = jnp.sum(jnp.where(hit, to_col(mean), 0.0), axis=0, keepdims=True)
    innovation = value_ref[...] - observed_mean
    which = iota((16, n), 0)
    last = jnp.where(which == 0, innovation, jnp.where(which == 1, prec_ref[...], 0.0)).astype(BF16)
    for ref, at in ((head_ref, 0), (tail_ref, n // 2)):
        ref[:members, :] = rows[:, at : at + n // 2]
        ref[members:, :] = last[:, at : at + n // 2]


def own_kernel(local_ref, y_ref, anomaly_ref, yt_ref, mean_ref, gram_ref, cover_ref):
    members, cells = local_ref.shape
    local = local_ref[...].astype(F32)
    mean = jnp.sum(local, axis=0, keepdims=True) * (1.0 / members)
    mean_ref[...] = jnp.broadcast_to(mean, mean_ref.shape)
    anomaly_ref[...] = (local - mean).astype(BF16)
    yt_ref[...] = y_ref[...].T
    gram_ref[...] = jnp.dot(yt_ref[...], y_ref[...], preferred_element_type=F32)
    cover_ref[...] = jnp.dot(yt_ref[...], anomaly_ref[...], preferred_element_type=F32)


def analyse_kernel(
    mask_ref, anomaly_ref, y_ref, yt_ref, mean_ref, gram_ref, cover_ref, left_ref, right_ref,
    index_ref, value_ref, prec_ref, out_ref, z, zt, gram, cover, u,
):
    members, cells = anomaly_ref.shape
    half = cells // 2
    quarter = half // 2
    n = index_ref.shape[1]

    z[:, :half] = y_ref[...]
    z[:, half : half + quarter] = left_ref[:members, :]
    z[:, half + quarter :] = right_ref[:members, :]
    zt[:half, :] = yt_ref[...]
    zt[half:, :] = z[:, half:].T
    rim = jnp.dot(zt[half:, :], z[...], preferred_element_type=F32)
    cross = jnp.dot(yt_ref[...], z[:, half:], preferred_element_type=F32)
    gram[:half, :half] = gram_ref[...]
    gram[:half, half:] = cross
    gram[half:, :] = rim
    cover[:half, :] = cover_ref[...]
    cover[half:, :] = jnp.dot(zt[half:, :], anomaly_ref[...], preferred_element_type=F32)

    mask = [mask_ref[0, b].astype(F32) for b in range(4)]
    hit = iota((half, n), 0) == index_ref[...]
    mean = mean_ref[0:1, :]
    cell_mean = to_col(mean[:, half:] + OBS_WIND * mean[:, :half])
    observed_mean = jnp.sum(jnp.where(hit, cell_mean, 0.0), axis=0, keepdims=True)
    innovation = (value_ref[...] - observed_mean).astype(BF16).astype(F32)
    weight = prec_ref[...].astype(BF16).astype(F32) * jnp.where(iota((1, n), 1) < n // 2, mask[1], mask[2])
    own_d = jnp.sum(jnp.where(hit, weight, 0.0), axis=1, keepdims=True)
    own_g = jnp.sum(jnp.where(hit, weight * innovation, 0.0), axis=1, keepdims=True)
    left_tail = left_ref[members : members + 16, :].astype(F32)
    right_tail = right_ref[members : members + 16, :].astype(F32)
    left_d = left_tail[1:2, :] * (0.5 * mask[0])
    right_d = right_tail[1:2, :] * (0.5 * mask[3])
    left_g = left_d * left_tail[0:1, :]
    right_g = right_d * right_tail[0:1, :]
    d_row = jnp.concatenate([to_row(own_d), left_d, right_d], axis=1)
    g_row = jnp.concatenate([to_row(own_g), left_g, right_g], axis=1)
    d_col = jnp.concatenate([own_d, to_col(left_d), to_col(right_d)], axis=0)
    g_col = jnp.concatenate([own_g, to_col(left_g), to_col(right_g)], axis=0)

    k = gram[...]
    m = cover[...]
    inner = (k * d_col * d_row).astype(BF16)
    u[...] = jnp.dot(z[...], inner, preferred_element_type=F32).astype(BF16)
    most = jnp.zeros((1, 1), F32)
    step = 256
    for i in range(members // step):
        squared = jnp.dot(u[i * step : (i + 1) * step, :], zt[...], preferred_element_type=F32)
        total = jnp.sum(jnp.abs(squared), axis=1, keepdims=True)
        most = jnp.maximum(most, jnp.max(total, axis=0, keepdims=True))
    row_bound = jnp.sqrt(most)
    half_width = (row_bound + 1.0) / 2.0
    theta = 1.0 + half_width
    ratio_sigma = theta / half_width
    rho_first = 1.0 / ratio_sigma
    rho_second = 1.0 / (2.0 * ratio_sigma - rho_first)
    resid_one = 1.0 - 1.0 / theta
    step_one = resid_one / theta
    step_cross = -1.0 / (theta * theta)
    second_one = resid_one - step_one
    second_cross = -1.0 / theta - step_cross - (theta - 1.0) / (theta * theta)
    first_rate = rho_second * rho_first
    second_rate = 2.0 * rho_second / half_width
    to_one = 1.0 / theta + step_one + first_rate * step_one + second_rate * second_one
    to_cross = step_cross + first_rate * step_cross + second_rate * second_cross
    to_square = second_rate / (theta * theta)

    dm = m * d_col
    kdm = jnp.dot(k.astype(BF16), dm.astype(BF16), preferred_element_type=F32)
    gain = (0.5 * to_cross * dm + (0.5 * to_square * d_col) * kdm).astype(BF16)
    once_row = d_row * jnp.sum(k * g_col, axis=0, keepdims=True)
    once_col = d_col * jnp.sum(k * g_row, axis=1, keepdims=True)
    twice_col = d_col * jnp.sum(k * once_row, axis=1, keepdims=True)
    force = to_one * g_col + to_cross * once_col + to_square * twice_col
    shift = mean + jnp.sum(force * m, axis=0, keepdims=True) * (members - 1) ** (-0.5)
    keep = 0.5 * (1.0 + to_one)
    for i in range(members // step):
        at = pl.ds(i * step, step)
        out_ref[at, :] = (
            shift
            + keep * anomaly_ref[at, :].astype(F32)
            + jnp.dot(z[at, :], gain, preferred_element_type=F32)
        ).astype(BF16)


def on_device(ensemble, obs_value, obs_prec, obs_row, obs_col, loc_mask):
    members, fields, rows, cols = ensemble.shape
    bands = lax.axis_size("member")
    domains = lax.axis_size("domain")
    total = members * bands
    cells = fields * (rows // bands) * cols
    n = obs_value.shape[1]
    to_right = [(i, (i + 1) % domains) for i in range(domains)]
    to_left = [((i + 1) % domains, i) for i in range(domains)]
    struct = jax.ShapeDtypeStruct

    edge = struct((8, members // 8 * fields * rows), F32)
    head, tail = call(edge_kernel, [edge, edge], [ensemble])
    west = lax.ppermute(tail, "domain", to_right)
    east = lax.ppermute(head, "domain", to_left)
    predicted = call(
        forecast_kernel,
        struct((bands, members, cells), BF16),
        [ensemble, west, east],
        scratch=[pltpu.VMEM((fields, members * rows, cols), F32)],
    )
    local = lax.all_to_all(predicted, "member", split_axis=0, concat_axis=0, tiled=True).reshape(total, cells)

    index = obs_row * cols + obs_col
    rim = struct((total + 16, n // 2), BF16)
    y, head_rows, tail_rows = call(
        observe_kernel,
        [struct((total, cells // 2), BF16), rim, rim],
        [local, index, obs_value, obs_prec],
    )
    left = lax.ppermute(tail_rows, "domain", to_right)
    right = lax.ppermute(head_rows, "domain", to_left)
    anomalies, yt, mean, gram, cover = call(
        own_kernel,
        [
            struct((total, cells), BF16),
            struct((cells // 2, total), BF16),
            struct((8, cells), F32),
            struct((cells // 2, cells // 2), F32),
            struct((cells // 2, cells), F32),
        ],
        [local, y],
        flops=2 * total * cells * cells * 3 // 4,
    )
    analysis = call(
        analyse_kernel,
        struct((total, cells), BF16),
        [loc_mask, anomalies, y, yt, mean, gram, cover, left, right, index, obs_value, obs_prec],
        scratch=[
            pltpu.VMEM((total, cells), BF16),
            pltpu.VMEM((cells, total), BF16),
            pltpu.VMEM((cells, cells), F32),
            pltpu.VMEM((cells, cells), F32),
            pltpu.VMEM((total, cells), BF16),
        ],
        specs=[SMEM] + [VMEM] * 11,
        flops=2 * total * total * cells * 2,
    )
    back = lax.all_to_all(
        analysis.reshape(bands, members, cells), "member", split_axis=0, concat_axis=0, tiled=True
    )
    return call(
        restore_kernel,
        struct(ensemble.shape, BF16),
        [back],
        scratch=[pltpu.VMEM((fields, members * rows, cols), F32)],
    )


def solution(mesh):
    in_specs = (
        P("member", None, None, "domain"),
        P("member", "domain"),
        P("member", "domain"),
        P("member", "domain"),
        P("member", "domain"),
        P("member", "domain"),
    )
    out_specs = P("member", None, None, "domain")
    return jax.shard_map(
        on_device, mesh=mesh, in_specs=in_specs, out_specs=out_specs, check_vma=False
    )
```

```python
import jax
import jax.numpy as jnp
from jax import lax
from jax.experimental import pallas as pl
from jax.experimental.pallas import tpu as pltpu
from jax.sharding import PartitionSpec as P

ADVECT = 0.4
DIFFUSE = 0.15
OBS_WIND = 0.5
F32 = jnp.float32
BF16 = jnp.bfloat16
VMEM = pl.BlockSpec(memory_space=pltpu.VMEM)
SMEM = pl.BlockSpec(memory_space=pltpu.SMEM)
PARAMS = pltpu.CompilerParams(vmem_limit_bytes=40 * 1024 * 1024)


def call(kernel, shapes, args, scratch=(), specs=None, flops=0):
    nbytes = sum(a.size * a.dtype.itemsize for a in args)
    return pl.pallas_call(
        kernel,
        out_shape=shapes,
        in_specs=specs or [VMEM] * len(args),
        out_specs=jax.tree.map(lambda _: VMEM, shapes),
        scratch_shapes=list(scratch),
        compiler_params=PARAMS,
        cost_estimate=pl.CostEstimate(flops=flops, bytes_accessed=nbytes, transcendentals=0),
    )(*args)


def iota(shape, dim):
    return lax.broadcasted_iota(jnp.int32, shape, dim)


def to_col(row):
    n = row.shape[1]
    return jnp.sum(jnp.where(iota((n, n), 0) == iota((n, n), 1), row, 0.0), axis=1, keepdims=True)


def to_row(col):
    n = col.shape[0]
    return jnp.sum(jnp.where(iota((n, n), 0) == iota((n, n), 1), col, 0.0), axis=0, keepdims=True)


def split_kernel(half_ref, ens_ref, near_ref, far_ref, head_ref, tail_ref, store):
    members, fields, rows, cols = ens_ref.shape
    slabs = members * fields
    part = rows // 2
    half = half_ref[0, 0]
    for ref, at in ((far_ref, 1 - half), (near_ref, half)):
        start = pl.multiple_of(at * part, part)
        ref[: slabs * part, :] = ens_ref[:, :, pl.ds(start, part), :].reshape(slabs * part, cols)
    store[...] = ens_ref[...].reshape(slabs * rows, cols).astype(F32)
    lines = [store[pl.ds(r, slabs, stride=rows), :].astype(BF16) for r in (part, rows - 1, 0, part - 1)]
    top, bottom = slabs * part, slabs * part + slabs
    low = [jnp.where(half == 0, lines[0], lines[2]), jnp.where(half == 0, lines[1], lines[3])]
    high = [jnp.where(half == 0, lines[2], lines[0]), jnp.where(half == 0, lines[3], lines[1])]
    for ref, (north, south) in ((far_ref, high), (near_ref, low)):
        ref[top : top + slabs, :] = north
        ref[bottom : bottom + slabs, :] = south
    spot, lane = iota((8, cols), 0), iota((8, cols), 1)
    pick = jnp.where((spot == 0) & (lane == 0) | (spot == 1) & (lane == cols - 1), 1.0, 0.0).astype(BF16)
    group = members // 8
    for k in range(8):
        lines = ens_ref[k * group : (k + 1) * group].reshape(-1, cols)
        edges = lax.dot_general(pick, lines, (((1,), (1,)), ((), ())), preferred_element_type=F32)
        head_ref[k : k + 1, :] = edges[0:1]
        tail_ref[k : k + 1, :] = edges[1:2]


def forecast_kernel(half_ref, block_ref, west_ref, east_ref, out_ref, halo, store):
    bands, members, _ = out_ref.shape
    cols = block_ref.shape[1]
    slabs = members * 2
    part = bands * 2
    rows = part * 2
    group = members // 8
    half = half_ref[0, 0]
    halo[...] = block_ref[slabs * part :, :].astype(F32)
    spot, lane8 = iota((8, cols), 0), iota((8, cols), 1)
    pick = jnp.where((spot == 0) & (lane8 == 0) | (spot == 1) & (lane8 == cols - 1), 1.0, 0.0).astype(BF16)
    lane, line = iota((part, cols), 1), iota((part, cols), 0)

    for k in range(8):
        n = group * 2 * rows
        which = iota((8, n), 0)
        edges = jnp.where(which == 0, west_ref[k : k + 1, :], jnp.where(which == 1, east_ref[k : k + 1, :], 0.0))
        rim = lax.dot_general(
            edges.astype(BF16), pick, (((0,), (0,)), ((), ())), preferred_element_type=F32
        ).reshape(group * 2, rows, cols)
        rim = jnp.where(half == 0, rim[:, :part], rim[:, part:])
        for i in range(group):
            m = k * group + i
            wind = None
            for f in range(2):
                s = m * 2 + f
                x = block_ref[s * part : (s + 1) * part, :].astype(F32)
                edge = rim[i * 2 + f]
                east = jnp.where(lane == cols - 1, edge, pltpu.roll(x, cols - 1, 1))
                west = jnp.where(lane == 0, edge, pltpu.roll(x, 1, 1))
                north = jnp.where(line == part - 1, halo[s : s + 1, :], pltpu.roll(x, part - 1, 0))
                south = jnp.where(line == 0, halo[slabs + s : slabs + s + 1, :], pltpu.roll(x, 1, 0))
                if f == 0:
                    wind = x
                laplace = east + west + north + south - 4.0 * x
                new = x - ADVECT * 0.5 * wind * (east - west) + DIFFUSE * laplace
                store[f, m * part : (m + 1) * part, :] = new
    for f in range(2):
        for r in range(part):
            line_r = store[f, pl.ds(r, members, stride=part), :]
            at = (f * 2 + r % 2) * cols
            out_ref[r // 2, :, at : at + cols] = line_r.astype(BF16)


def restore_kernel(in_ref, out_ref, store):
    members, _, rows, cols = out_ref.shape
    for f in range(2):
        for r in range(rows):
            at = (f * 2 + r % 2) * cols
            store[f, pl.ds(r, members, stride=rows), :] = in_ref[r // 2, :, at : at + cols].astype(F32)
    for f in range(2):
        for m in range(members):
            out_ref[m, f] = store[f, m * rows : (m + 1) * rows, :].astype(BF16)


def observe_kernel(near_ref, far_ref, index_ref, value_ref, prec_ref, y_ref, head_ref, tail_ref):
    local = jnp.concatenate([near_ref[...], far_ref[...]], axis=0).astype(F32)
    members, cells = local.shape
    half = cells // 2
    equivalent = local[:, half:] + OBS_WIND * local[:, :half]
    mean = jnp.sum(equivalent, axis=0, keepdims=True) * (1.0 / members)
    y = ((equivalent - mean) * (members - 1) ** (-0.5)).astype(BF16)
    y_ref[...] = y
    n = index_ref.shape[1]
    hit = iota((half, n), 0) == index_ref[...]
    rows = jnp.dot(y, hit.astype(BF16), preferred_element_type=F32).astype(BF16)
    observed_mean = jnp.sum(jnp.where(hit, to_col(mean), 0.0), axis=0, keepdims=True)
    innovation = value_ref[...] - observed_mean
    which = iota((16, n), 0)
    last = jnp.where(which == 0, innovation, jnp.where(which == 1, prec_ref[...], 0.0)).astype(BF16)
    for ref, at in ((head_ref, 0), (tail_ref, n // 2)):
        ref[:members, :] = rows[:, at : at + n // 2]
        ref[members:, :] = last[:, at : at + n // 2]


def own_kernel(near_ref, far_ref, y_ref, anomaly_ref, yt_ref, mean_ref, gram_ref, cover_ref):
    local = jnp.concatenate([near_ref[...], far_ref[...]], axis=0).astype(F32)
    members, cells = local.shape
    mean = jnp.sum(local, axis=0, keepdims=True) * (1.0 / members)
    mean_ref[...] = jnp.broadcast_to(mean, mean_ref.shape)
    anomaly_ref[...] = (local - mean).astype(BF16)
    yt_ref[...] = y_ref[...].T
    gram_ref[...] = jnp.dot(yt_ref[...], y_ref[...], preferred_element_type=F32)
    cover_ref[...] = jnp.dot(yt_ref[...], anomaly_ref[...], preferred_element_type=F32)


def analyse_kernel(
    mask_ref, half_ref, anomaly_ref, y_ref, yt_ref, mean_ref, gram_ref, cover_ref, left_ref, right_ref,
    index_ref, value_ref, prec_ref, out_ref, z, zt, gram, cover, u,
):
    members, cells = anomaly_ref.shape
    half = cells // 2
    quarter = half // 2
    n = index_ref.shape[1]

    z[:, :half] = y_ref[...]
    z[:, half : half + quarter] = left_ref[:members, :]
    z[:, half + quarter :] = right_ref[:members, :]
    zt[:half, :] = yt_ref[...]
    zt[half:, :] = z[:, half:].T
    rim = jnp.dot(zt[half:, :], z[...], preferred_element_type=F32)
    cross = jnp.dot(yt_ref[...], z[:, half:], preferred_element_type=F32)
    gram[:half, :half] = gram_ref[...]
    gram[:half, half:] = cross
    gram[half:, :] = rim
    cover[:half, :] = cover_ref[...]
    cover[half:, :] = jnp.dot(zt[half:, :], anomaly_ref[...], preferred_element_type=F32)

    mask = [mask_ref[0:1, b : b + 1].astype(F32) for b in range(4)]
    hit = iota((half, n), 0) == index_ref[...]
    mean = mean_ref[0:1, :]
    cell_mean = to_col(mean[:, half:] + OBS_WIND * mean[:, :half])
    observed_mean = jnp.sum(jnp.where(hit, cell_mean, 0.0), axis=0, keepdims=True)
    innovation = (value_ref[...] - observed_mean).astype(BF16).astype(F32)
    weight = prec_ref[...].astype(BF16).astype(F32) * jnp.where(iota((1, n), 1) < n // 2, mask[1], mask[2])
    own_d = jnp.sum(jnp.where(hit, weight, 0.0), axis=1, keepdims=True)
    own_g = jnp.sum(jnp.where(hit, weight * innovation, 0.0), axis=1, keepdims=True)
    left_tail = left_ref[members : members + 16, :].astype(F32)
    right_tail = right_ref[members : members + 16, :].astype(F32)
    left_d = left_tail[1:2, :] * (0.5 * mask[0])
    right_d = right_tail[1:2, :] * (0.5 * mask[3])
    left_g = left_d * left_tail[0:1, :]
    right_g = right_d * right_tail[0:1, :]
    d_row = jnp.concatenate([to_row(own_d), left_d, right_d], axis=1)
    g_row = jnp.concatenate([to_row(own_g), left_g, right_g], axis=1)
    d_col = jnp.concatenate([own_d, to_col(left_d), to_col(right_d)], axis=0)
    g_col = jnp.concatenate([own_g, to_col(left_g), to_col(right_g)], axis=0)

    k = gram[...]
    m = cover[...]
    inner = (k * d_col * d_row).astype(BF16)
    u[...] = jnp.dot(z[...], inner, preferred_element_type=F32).astype(BF16)
    most = jnp.zeros((1, 1), F32)
    step = 256
    for i in range(members // step):
        squared = jnp.dot(u[i * step : (i + 1) * step, :], zt[...], preferred_element_type=F32)
        total = jnp.sum(jnp.abs(squared), axis=1, keepdims=True)
        most = jnp.maximum(most, jnp.max(total, axis=0, keepdims=True))
    row_bound = jnp.sqrt(most)
    half_width = (row_bound + 1.0) / 2.0
    theta = 1.0 + half_width
    ratio_sigma = theta / half_width
    rho_first = 1.0 / ratio_sigma
    rho_second = 1.0 / (2.0 * ratio_sigma - rho_first)
    resid_one = 1.0 - 1.0 / theta
    step_one = resid_one / theta
    step_cross = -1.0 / (theta * theta)
    second_one = resid_one - step_one
    second_cross = -1.0 / theta - step_cross - (theta - 1.0) / (theta * theta)
    first_rate = rho_second * rho_first
    second_rate = 2.0 * rho_second / half_width
    to_one = 1.0 / theta + step_one + first_rate * step_one + second_rate * second_one
    to_cross = step_cross + first_rate * step_cross + second_rate * second_cross
    to_square = second_rate / (theta * theta)

    dm = m * d_col
    kdm = jnp.dot(k.astype(BF16), dm.astype(BF16), preferred_element_type=F32)
    gain = (0.5 * to_cross * dm + (0.5 * to_square * d_col) * kdm).astype(BF16)
    once_row = d_row * jnp.sum(k * g_col, axis=0, keepdims=True)
    once_col = d_col * jnp.sum(k * g_row, axis=1, keepdims=True)
    twice_col = d_col * jnp.sum(k * once_row, axis=1, keepdims=True)
    force = to_one * g_col + to_cross * once_col + to_square * twice_col
    shift = mean + jnp.sum(force * m, axis=0, keepdims=True) * (members - 1) ** (-0.5)
    keep = 0.5 * (1.0 + to_one)
    for i in range(members // step):
        at = pl.ds(i * step, step)
        side = i * step // (members // 2)
        side = side + half_ref[0, 0] * (1 - 2 * side)
        out_ref[side, pl.ds(i * step % (members // 2), step), :] = (
            shift
            + keep * anomaly_ref[at, :].astype(F32)
            + jnp.dot(z[at, :], gain, preferred_element_type=F32)
        ).astype(BF16)


def on_device(ensemble, obs_value, obs_prec, obs_row, obs_col, loc_mask):
    members, fields, rows, cols = ensemble.shape
    bands = lax.axis_size("member")
    domains = lax.axis_size("domain")
    total = members * bands
    cells = fields * (rows // bands) * cols
    n = obs_value.shape[1]
    to_right = [(i, (i + 1) % domains) for i in range(domains)]
    to_left = [((i + 1) % domains, i) for i in range(domains)]
    struct = jax.ShapeDtypeStruct

    part = bands // 2
    half = (lax.axis_index("member") // part).astype(jnp.int32).reshape(1, 1)
    groups = [[g * part + i for i in range(part)] for g in range(2)]
    swap = [(i, (i + part) % bands) for i in range(bands)]
    lines = members * fields * (rows // 2 + 2)

    edge = struct((8, members // 8 * fields * rows), F32)
    block = struct((lines, cols), BF16)
    near, far, head, tail = call(
        split_kernel,
        [block, block, edge, edge],
        [half, ensemble],
        scratch=[pltpu.VMEM((members * fields * rows, cols), F32)],
        specs=[SMEM, VMEM],
    )
    far = lax.ppermute(far, "member", swap)
    west = lax.ppermute(tail, "domain", to_right)
    east = lax.ppermute(head, "domain", to_left)
    far_edges = lax.ppermute(jnp.concatenate([west, east], axis=0), "member", swap)

    def forecast(rows_of, west_of, east_of):
        predicted = call(
            forecast_kernel,
            struct((part, members, cells), BF16),
            [half, rows_of, west_of, east_of],
            scratch=[
                pltpu.VMEM((2 * members * fields, cols), F32),
                pltpu.VMEM((fields, members * rows // 2, cols), F32),
            ],
            specs=[SMEM, VMEM, VMEM, VMEM],
        )
        return lax.all_to_all(
            predicted, "member", split_axis=0, concat_axis=0, axis_index_groups=groups, tiled=True
        ).reshape(total // 2, cells)

    near_local = forecast(near, west, east)
    far_local = forecast(far, far_edges[:8], far_edges[8:])

    index = obs_row * cols + obs_col
    rim = struct((total + 16, n // 2), BF16)
    y, head_rows, tail_rows = call(
        observe_kernel,
        [struct((total, cells // 2), BF16), rim, rim],
        [near_local, far_local, index, obs_value, obs_prec],
    )
    left = lax.ppermute(tail_rows, "domain", to_right)
    right = lax.ppermute(head_rows, "domain", to_left)
    anomalies, yt, mean, gram, cover = call(
        own_kernel,
        [
            struct((total, cells), BF16),
            struct((cells // 2, total), BF16),
            struct((8, cells), F32),
            struct((cells // 2, cells // 2), F32),
            struct((cells // 2, cells), F32),
        ],
        [near_local, far_local, y],
        flops=2 * total * cells * cells * 3 // 4,
    )
    analysis = call(
        analyse_kernel,
        struct((2, total // 2, cells), BF16),
        [loc_mask, half, anomalies, y, yt, mean, gram, cover, left, right, index, obs_value, obs_prec],
        scratch=[
            pltpu.VMEM((total, cells), BF16),
            pltpu.VMEM((cells, total), BF16),
            pltpu.VMEM((cells, cells), F32),
            pltpu.VMEM((cells, cells), F32),
            pltpu.VMEM((total, cells), BF16),
        ],
        specs=[VMEM, SMEM] + [VMEM] * 11,
        flops=2 * total * total * cells * 2,
    )
    back = lax.all_to_all(
        analysis.reshape(bands, members, cells), "member", split_axis=0, concat_axis=0, tiled=True
    )
    return call(
        restore_kernel,
        struct(ensemble.shape, BF16),
        [back],
        scratch=[pltpu.VMEM((fields, members * rows, cols), F32)],
    )


def solution(mesh):
    in_specs = (
        P("member", None, None, "domain"),
        P("member", "domain"),
        P("member", "domain"),
        P("member", "domain"),
        P("member", "domain"),
        P("member", "domain"),
    )
    out_specs = P("member", None, None, "domain")
    return jax.shard_map(
        on_device, mesh=mesh, in_specs=in_specs, out_specs=out_specs, check_vma=False
    )
```

```python
import jax
import jax.numpy as jnp
from jax import lax
from jax.experimental import pallas as pl
from jax.experimental.pallas import tpu as pltpu
from jax.sharding import PartitionSpec as P

ADVECT = 0.4
DIFFUSE = 0.15
OBS_WIND = 0.5
F32 = jnp.float32
BF16 = jnp.bfloat16
VMEM = pl.BlockSpec(memory_space=pltpu.VMEM)
SMEM = pl.BlockSpec(memory_space=pltpu.SMEM)
PARAMS = pltpu.CompilerParams(vmem_limit_bytes=40 * 1024 * 1024)


def call(kernel, shapes, args, scratch=(), specs=None, flops=0):
    nbytes = sum(a.size * a.dtype.itemsize for a in args)
    return pl.pallas_call(
        kernel,
        out_shape=shapes,
        in_specs=specs or [VMEM] * len(args),
        out_specs=jax.tree.map(lambda _: VMEM, shapes),
        scratch_shapes=list(scratch),
        compiler_params=PARAMS,
        cost_estimate=pl.CostEstimate(flops=flops, bytes_accessed=nbytes, transcendentals=0),
    )(*args)


def iota(shape, dim):
    return lax.broadcasted_iota(jnp.int32, shape, dim)


def to_col(row):
    n = row.shape[1]
    return jnp.sum(jnp.where(iota((n, n), 0) == iota((n, n), 1), row, 0.0), axis=1, keepdims=True)


def to_row(col):
    n = col.shape[0]
    return jnp.sum(jnp.where(iota((n, n), 0) == iota((n, n), 1), col, 0.0), axis=0, keepdims=True)


def edge_kernel(even_ref, ens_ref, pair_ref, cross_ref):
    pick = jnp.where(
        (iota((8, 128), 0) == 0) & (iota((8, 128), 1) == 0)
        | (iota((8, 128), 0) == 1) & (iota((8, 128), 1) == 127),
        1.0,
        0.0,
    ).astype(BF16)
    even = even_ref[0, 0] == 1
    members = ens_ref.shape[0] // 8
    for k in range(8):
        rows = ens_ref[k * members : (k + 1) * members].reshape(-1, 128)
        edges = lax.dot_general(pick, rows, (((1,), (1,)), ((), ())), preferred_element_type=F32)
        head, tail = edges[0:1], edges[1:2]
        pair_ref[k : k + 1, :] = jnp.where(even, tail, head)
        cross_ref[k : k + 1, :] = jnp.where(even, head, tail)


def inside_kernel(ens_ref, new_ref):
    members, _, rows, cols = ens_ref.shape
    lane = iota((rows, cols), 1)
    for m in range(members):
        wind = None
        for f in range(2):
            x = ens_ref[m, f].astype(F32)
            east = jnp.where(lane == cols - 1, 0.0, pltpu.roll(x, cols - 1, 1))
            west = jnp.where(lane == 0, 0.0, pltpu.roll(x, 1, 1))
            north = pltpu.roll(x, rows - 1, 0)
            south = pltpu.roll(x, 1, 0)
            if f == 0:
                wind = x
            laplace = east + west + north + south - 4.0 * x
            new_ref[f, m * rows : (m + 1) * rows, :] = x - ADVECT * 0.5 * wind * (east - west) + DIFFUSE * laplace


def forecast_kernel(even_ref, new_ref, ens_ref, pair_ref, cross_ref, out_ref, store):
    members, _, rows, cols = ens_ref.shape
    group = members // 8
    even = even_ref[0, 0] == 1
    spot = iota((8, cols), 0)
    lane8 = iota((8, cols), 1)
    pick = jnp.where((spot == 0) & (lane8 == 0) | (spot == 1) & (lane8 == cols - 1), 1.0, 0.0).astype(BF16)
    side = jnp.where(iota((rows, cols), 1) == 0, ADVECT * 0.5, -ADVECT * 0.5)

    for k in range(8):
        n = group * 2 * rows
        which = iota((8, n), 0)
        pair, cross = pair_ref[k : k + 1, :], cross_ref[k : k + 1, :]
        west, east = jnp.where(even, cross, pair), jnp.where(even, pair, cross)
        edges = jnp.where(which == 0, west, jnp.where(which == 1, east, 0.0))
        rim = lax.dot_general(
            edges.astype(BF16), pick, (((0,), (0,)), ((), ())), preferred_element_type=F32
        ).reshape(group * 2, rows, cols)
        for i in range(group):
            m = k * group + i
            rate = side * ens_ref[m, 0].astype(F32) + DIFFUSE
            for f in range(2):
                at = slice(m * rows, (m + 1) * rows)
                store[f, at, :] = new_ref[f, at, :] + rate * rim[i * 2 + f]
    for f in range(2):
        for r in range(rows):
            part = store[f, pl.ds(r, members, stride=rows), :]
            at = (f * 2 + r % 2) * cols
            out_ref[r // 2, :, at : at + cols] = part.astype(BF16)


def restore_kernel(in_ref, out_ref, store):
    members, _, rows, cols = out_ref.shape
    for f in range(2):
        for r in range(rows):
            at = (f * 2 + r % 2) * cols
            store[f, pl.ds(r, members, stride=rows), :] = in_ref[r // 2, :, at : at + cols].astype(F32)
    for f in range(2):
        for m in range(members):
            out_ref[m, f] = store[f, m * rows : (m + 1) * rows, :].astype(BF16)


def observe_kernel(even_ref, local_ref, index_ref, value_ref, prec_ref, y_ref, mean_ref, pair_ref, cross_ref):
    members, cells = local_ref.shape
    half = cells // 2
    equivalent = local_ref[:, half:].astype(F32) + OBS_WIND * local_ref[:, :half].astype(F32)
    mean = jnp.sum(equivalent, axis=0, keepdims=True) * (1.0 / members)
    mean_ref[...] = jnp.broadcast_to(mean, mean_ref.shape)
    y_ref[...] = ((equivalent - mean) * (members - 1) ** (-0.5)).astype(BF16)
    n = index_ref.shape[1] // 2
    even = even_ref[0, 0]
    for ref, side in ((cross_ref, 1 - even), (pair_ref, even)):
        at = pl.ds(pl.multiple_of(side * n, n), n)
        hit = iota((half, n), 0) == index_ref[:, at]
        ref[:members, :] = jnp.dot(y_ref[...], hit.astype(BF16), preferred_element_type=F32).astype(BF16)
        innovation = value_ref[:, at] - jnp.sum(jnp.where(hit, to_col(mean), 0.0), axis=0, keepdims=True)
        which = iota((16, n), 0)
        last = jnp.where(which == 0, innovation, jnp.where(which == 1, prec_ref[:, at], 0.0))
        ref[members:, :] = last.astype(BF16)


def own_kernel(
    mask_ref, local_ref, y_ref, observed_ref, index_ref, value_ref, prec_ref,
    anomaly_ref, yt_ref, mean_ref, gram_ref, cover_ref, row_ref, col_ref,
):
    members, cells = local_ref.shape
    half = cells // 2
    local = local_ref[...].astype(F32)
    mean = jnp.sum(local, axis=0, keepdims=True) * (1.0 / members)
    mean_ref[...] = jnp.broadcast_to(mean, mean_ref.shape)
    anomaly_ref[...] = (local - mean).astype(BF16)
    yt_ref[...] = y_ref[...].T
    gram_ref[...] = jnp.dot(yt_ref[...], y_ref[...], preferred_element_type=F32)
    cover_ref[...] = jnp.dot(yt_ref[...], anomaly_ref[...], preferred_element_type=F32)

    n = index_ref.shape[1]
    hit = iota((half, n), 0) == index_ref[...]
    observed_mean = jnp.sum(jnp.where(hit, to_col(observed_ref[0:1, :]), 0.0), axis=0, keepdims=True)
    innovation = (value_ref[...] - observed_mean).astype(BF16).astype(F32)
    mask = jnp.where(iota((1, n), 1) < n // 2, mask_ref[0:1, 1:2].astype(F32), mask_ref[0:1, 2:3].astype(F32))
    weight = prec_ref[...].astype(BF16).astype(F32) * mask
    own_d = jnp.sum(jnp.where(hit, weight, 0.0), axis=1, keepdims=True)
    own_g = jnp.sum(jnp.where(hit, weight * innovation, 0.0), axis=1, keepdims=True)
    which = iota((8, half), 0)
    row_ref[...] = jnp.where(which == 0, to_row(own_d), to_row(own_g))
    lane = iota((half, 128), 1)
    col_ref[...] = jnp.where(lane == 0, own_d, own_g)


def analyse_kernel(
    even_ref, mask_ref, anomaly_ref, y_ref, yt_ref, mean_ref, gram_ref, cover_ref, row_ref, col_ref,
    pair_ref, cross_ref, out_ref, z, zt, gram, cover, u,
):
    members, cells = anomaly_ref.shape
    half = cells // 2
    quarter = half // 2

    z[:, :half] = y_ref[...]
    z[:, half : half + quarter] = pair_ref[:members, :]
    z[:, half + quarter :] = cross_ref[:members, :]
    zt[:half, :] = yt_ref[...]
    zt[half:, :] = z[:, half:].T
    rim = jnp.dot(zt[half:, :], z[...], preferred_element_type=F32)
    cross = jnp.dot(yt_ref[...], z[:, half:], preferred_element_type=F32)
    gram[:half, :half] = gram_ref[...]
    gram[:half, half:] = cross
    gram[half:, :] = rim
    cover[:half, :] = cover_ref[...]
    cover[half:, :] = jnp.dot(zt[half:, :], anomaly_ref[...], preferred_element_type=F32)

    mean = mean_ref[0:1, :]
    even = even_ref[0, 0] == 1
    left_mask, right_mask = mask_ref[0:1, 0:1].astype(F32), mask_ref[0:1, 3:4].astype(F32)
    pair_tail = pair_ref[members : members + 16, :].astype(F32)
    cross_tail = cross_ref[members : members + 16, :].astype(F32)
    pair_d = pair_tail[1:2, :] * (0.5 * jnp.where(even, right_mask, left_mask))
    cross_d = cross_tail[1:2, :] * (0.5 * jnp.where(even, left_mask, right_mask))
    pair_g = pair_d * pair_tail[0:1, :]
    cross_g = cross_d * cross_tail[0:1, :]
    d_row = jnp.concatenate([row_ref[0:1, :], pair_d, cross_d], axis=1)
    g_row = jnp.concatenate([row_ref[1:2, :], pair_g, cross_g], axis=1)
    d_col = jnp.concatenate([col_ref[:, 0:1], to_col(pair_d), to_col(cross_d)], axis=0)
    g_col = jnp.concatenate([col_ref[:, 1:2], to_col(pair_g), to_col(cross_g)], axis=0)

    k = gram[...]
    m = cover[...]
    inner = (k * d_col * d_row).astype(BF16)
    u[...] = jnp.dot(z[...], inner, preferred_element_type=F32).astype(BF16)
    most = jnp.zeros((1, 1), F32)
    step = 256
    for i in range(members // step):
        squared = jnp.dot(u[i * step : (i + 1) * step, :], zt[...], preferred_element_type=F32)
        total = jnp.sum(jnp.abs(squared), axis=1, keepdims=True)
        most = jnp.maximum(most, jnp.max(total, axis=0, keepdims=True))
    row_bound = jnp.sqrt(most)
    half_width = (row_bound + 1.0) / 2.0
    theta = 1.0 + half_width
    ratio_sigma = theta / half_width
    rho_first = 1.0 / ratio_sigma
    rho_second = 1.0 / (2.0 * ratio_sigma - rho_first)
    resid_one = 1.0 - 1.0 / theta
    step_one = resid_one / theta
    step_cross = -1.0 / (theta * theta)
    second_one = resid_one - step_one
    second_cross = -1.0 / theta - step_cross - (theta - 1.0) / (theta * theta)
    first_rate = rho_second * rho_first
    second_rate = 2.0 * rho_second / half_width
    to_one = 1.0 / theta + step_one + first_rate * step_one + second_rate * second_one
    to_cross = step_cross + first_rate * step_cross + second_rate * second_cross
    to_square = second_rate / (theta * theta)

    dm = m * d_col
    kdm = jnp.dot(k.astype(BF16), dm.astype(BF16), preferred_element_type=F32)
    gain = (0.5 * to_cross * dm + (0.5 * to_square * d_col) * kdm).astype(BF16)
    once_row = d_row * jnp.sum(k * g_col, axis=0, keepdims=True)
    once_col = d_col * jnp.sum(k * g_row, axis=1, keepdims=True)
    twice_col = d_col * jnp.sum(k * once_row, axis=1, keepdims=True)
    force = to_one * g_col + to_cross * once_col + to_square * twice_col
    shift = mean + jnp.sum(force * m, axis=0, keepdims=True) * (members - 1) ** (-0.5)
    keep = 0.5 * (1.0 + to_one)
    for i in range(members // step):
        at = pl.ds(i * step, step)
        out_ref[at, :] = (
            shift
            + keep * anomaly_ref[at, :].astype(F32)
            + jnp.dot(z[at, :], gain, preferred_element_type=F32)
        ).astype(BF16)


def on_device(ensemble, obs_value, obs_prec, obs_row, obs_col, loc_mask):
    members, fields, rows, cols = ensemble.shape
    bands = lax.axis_size("member")
    domains = lax.axis_size("domain")
    total = members * bands
    cells = fields * (rows // bands) * cols
    n = obs_value.shape[1]
    pairs = [(i, i ^ 1) for i in range(domains)]
    crosses = [(i, (i - 1 + 2 * (i % 2)) % domains) for i in range(domains)]
    struct = jax.ShapeDtypeStruct
    even = (1 - lax.axis_index("domain") % 2).astype(jnp.int32).reshape(1, 1)

    edge = struct((8, members // 8 * fields * rows), F32)
    pair_edge, cross_edge = call(edge_kernel, [edge, edge], [even, ensemble], specs=[SMEM, VMEM])
    cross_edge = lax.ppermute(cross_edge, "domain", crosses)
    pair_edge = lax.ppermute(pair_edge, "domain", pairs)
    inside = call(inside_kernel, struct((fields, members * rows, cols), F32), [ensemble])
    predicted = call(
        forecast_kernel,
        struct((bands, members, cells), BF16),
        [even, inside, ensemble, pair_edge, cross_edge],
        scratch=[pltpu.VMEM((fields, members * rows, cols), F32)],
        specs=[SMEM] + [VMEM] * 4,
    )
    local = lax.all_to_all(predicted, "member", split_axis=0, concat_axis=0, tiled=True).reshape(total, cells)

    index = obs_row * cols + obs_col
    rim = struct((total + 16, n // 2), BF16)
    y, observed, pair_rows, cross_rows = call(
        observe_kernel,
        [struct((total, cells // 2), BF16), struct((8, cells // 2), F32), rim, rim],
        [even, local, index, obs_value, obs_prec],
        specs=[SMEM] + [VMEM] * 4,
    )
    cross_rows = lax.ppermute(cross_rows, "domain", crosses)
    pair_rows = lax.ppermute(pair_rows, "domain", pairs)
    own = call(
        own_kernel,
        [
            struct((total, cells), BF16),
            struct((cells // 2, total), BF16),
            struct((8, cells), F32),
            struct((cells // 2, cells // 2), F32),
            struct((cells // 2, cells), F32),
            struct((8, cells // 2), F32),
            struct((cells // 2, 128), F32),
        ],
        [loc_mask, local, y, observed, index, obs_value, obs_prec],
        flops=2 * total * cells * cells * 3 // 4,
    )
    anomalies, yt, mean, gram, cover, row, col = own
    analysis = call(
        analyse_kernel,
        struct((total, cells), BF16),
        [even, loc_mask, anomalies, y, yt, mean, gram, cover, row, col, pair_rows, cross_rows],
        scratch=[
            pltpu.VMEM((total, cells), BF16),
            pltpu.VMEM((cells, total), BF16),
            pltpu.VMEM((cells, cells), F32),
            pltpu.VMEM((cells, cells), F32),
            pltpu.VMEM((total, cells), BF16),
        ],
        specs=[SMEM] + [VMEM] * 11,
        flops=2 * total * total * cells * 2,
    )
    back = lax.all_to_all(
        analysis.reshape(bands, members, cells), "member", split_axis=0, concat_axis=0, tiled=True
    )
    return call(
        restore_kernel,
        struct(ensemble.shape, BF16),
        [back],
        scratch=[pltpu.VMEM((fields, members * rows, cols), F32)],
    )


def solution(mesh):
    in_specs = (
        P("member", None, None, "domain"),
        P("member", "domain"),
        P("member", "domain"),
        P("member", "domain"),
        P("member", "domain"),
        P("member", "domain"),
    )
    out_specs = P("member", None, None, "domain")
    return jax.shard_map(
        on_device, mesh=mesh, in_specs=in_specs, out_specs=out_specs, check_vma=False
    )
```

```python
import jax
import jax.numpy as jnp
from jax import lax
from jax.experimental import pallas as pl
from jax.experimental.pallas import tpu as pltpu
from jax.sharding import PartitionSpec as P

ADVECT = 0.4
DIFFUSE = 0.15
OBS_WIND = 0.5
SKEW = 4
F32 = jnp.float32
BF16 = jnp.bfloat16
VMEM = pl.BlockSpec(memory_space=pltpu.VMEM)
SMEM = pl.BlockSpec(memory_space=pltpu.SMEM)
PARAMS = pltpu.CompilerParams(vmem_limit_bytes=40 * 1024 * 1024)


def call(kernel, shapes, args, scratch=(), specs=None, flops=0):
    nbytes = sum(a.size * a.dtype.itemsize for a in args)
    return pl.pallas_call(
        kernel,
        out_shape=shapes,
        in_specs=specs or [VMEM] * len(args),
        out_specs=jax.tree.map(lambda _: VMEM, shapes),
        scratch_shapes=list(scratch),
        compiler_params=PARAMS,
        cost_estimate=pl.CostEstimate(flops=flops, bytes_accessed=nbytes, transcendentals=0),
    )(*args)


def iota(shape, dim):
    return lax.broadcasted_iota(jnp.int32, shape, dim)


def to_col(row):
    n = row.shape[1]
    return jnp.sum(jnp.where(iota((n, n), 0) == iota((n, n), 1), row, 0.0), axis=1, keepdims=True)


def to_row(col):
    n = col.shape[0]
    return jnp.sum(jnp.where(iota((n, n), 0) == iota((n, n), 1), col, 0.0), axis=0, keepdims=True)


def write_edges(ens_ref, tail, edge_ref):
    rows, cols = ens_ref.shape[2:]
    pick = (iota((8, cols), 1) == jnp.where(tail, cols - 1, 0)).astype(F32).astype(BF16)
    members = ens_ref.shape[0] // 8
    for k in range(8):
        lines = ens_ref[k * members : (k + 1) * members].reshape(-1, cols)
        edges = lax.dot_general(pick, lines, (((1,), (1,)), ((), ())), preferred_element_type=F32)
        edge_ref[k : k + 1, :] = edges[0:1]


def edge_kernel(even_ref, ens_ref, cross_ref):
    write_edges(ens_ref, even_ref[0, 0] == 0, cross_ref)


def inside_kernel(even_ref, ens_ref, pair_ref, new_ref):
    members, _, rows, cols = ens_ref.shape
    write_edges(ens_ref, even_ref[0, 0] == 1, pair_ref)
    lane = iota((rows, cols), 1)
    for m in range(members):
        wind = None
        for f in range(2):
            x = ens_ref[m, f].astype(F32)
            east = jnp.where(lane == cols - 1, 0.0, pltpu.roll(x, cols - 1, 1))
            west = jnp.where(lane == 0, 0.0, pltpu.roll(x, 1, 1))
            north = pltpu.roll(x, rows - 1, 0)
            south = pltpu.roll(x, 1, 0)
            if f == 0:
                wind = x
            laplace = east + west + north + south - 4.0 * x
            new_ref[f, m * rows : (m + 1) * rows, :] = x - ADVECT * 0.5 * wind * (east - west) + DIFFUSE * laplace


def forecast_kernel(even_ref, new_ref, ens_ref, pair_ref, cross_ref, out_ref, store):
    members, _, rows, cols = ens_ref.shape
    group = members // 8
    pitch = store.shape[1] // members
    even = even_ref[0, 0] == 1
    spot = iota((8, cols), 0)
    lane8 = iota((8, cols), 1)
    pick = jnp.where((spot == 0) & (lane8 == 0) | (spot == 1) & (lane8 == cols - 1), 1.0, 0.0).astype(BF16)
    side = jnp.where(iota((rows, cols), 1) == 0, ADVECT * 0.5, -ADVECT * 0.5)

    for k in range(8):
        n = group * 2 * rows
        which = iota((8, n), 0)
        pair, cross = pair_ref[k : k + 1, :], cross_ref[k : k + 1, :]
        west, east = jnp.where(even, cross, pair), jnp.where(even, pair, cross)
        edges = jnp.where(which == 0, west, jnp.where(which == 1, east, 0.0))
        rim = lax.dot_general(
            edges.astype(BF16), pick, (((0,), (0,)), ((), ())), preferred_element_type=F32
        ).reshape(group * 2, rows, cols)
        for i in range(group):
            m = k * group + i
            rate = side * ens_ref[m, 0].astype(F32) + DIFFUSE
            for f in range(2):
                at = slice(m * rows, (m + 1) * rows)
                store[f, m * pitch : m * pitch + rows, :] = new_ref[f, at, :] + rate * rim[i * 2 + f]
    for f in range(2):
        for r in range(rows):
            part = store[f, pl.ds(r, members, stride=pitch), :]
            at = (f * 2 + r % 2) * cols
            out_ref[r // 2, :, at : at + cols] = part.astype(BF16)


def restore_kernel(in_ref, out_ref, store):
    members, _, rows, cols = out_ref.shape
    pitch = store.shape[1] // members
    for f in range(2):
        for r in range(rows):
            at = (f * 2 + r % 2) * cols
            store[f, pl.ds(r, members, stride=pitch), :] = in_ref[r // 2, :, at : at + cols].astype(F32)
    for f in range(2):
        for m in range(members):
            out_ref[m, f] = store[f, m * pitch : m * pitch + rows, :].astype(BF16)


def write_rows(side, y_ref, mean, index_ref, value_ref, prec_ref, ref):
    members, half = y_ref.shape
    n = index_ref.shape[1] // 2
    at = pl.ds(pl.multiple_of(side * n, n), n)
    hit = iota((half, n), 0) == index_ref[:, at]
    ref[:members, :] = jnp.dot(y_ref[...], hit.astype(BF16), preferred_element_type=F32).astype(BF16)
    innovation = value_ref[:, at] - jnp.sum(jnp.where(hit, to_col(mean), 0.0), axis=0, keepdims=True)
    which = iota((16, n), 0)
    last = jnp.where(which == 0, innovation, jnp.where(which == 1, prec_ref[:, at], 0.0))
    ref[members:, :] = last.astype(BF16)


def observe_kernel(even_ref, local_ref, index_ref, value_ref, prec_ref, y_ref, mean_ref, cross_ref):
    members, cells = local_ref.shape
    half = cells // 2
    equivalent = local_ref[:, half:].astype(F32) + OBS_WIND * local_ref[:, :half].astype(F32)
    mean = jnp.sum(equivalent, axis=0, keepdims=True) * (1.0 / members)
    mean_ref[...] = jnp.broadcast_to(mean, mean_ref.shape)
    y_ref[...] = ((equivalent - mean) * (members - 1) ** (-0.5)).astype(BF16)
    write_rows(1 - even_ref[0, 0], y_ref, mean, index_ref, value_ref, prec_ref, cross_ref)


def own_kernel(
    even_ref, mask_ref, local_ref, y_ref, observed_ref, index_ref, value_ref, prec_ref,
    pair_ref, anomaly_ref, yt_ref, mean_ref, gram_ref, cover_ref, row_ref, col_ref,
):
    write_rows(even_ref[0, 0], y_ref, observed_ref[0:1, :], index_ref, value_ref, prec_ref, pair_ref)
    members, cells = local_ref.shape
    half = cells // 2
    local = local_ref[...].astype(F32)
    mean = jnp.sum(local, axis=0, keepdims=True) * (1.0 / members)
    mean_ref[...] = jnp.broadcast_to(mean, mean_ref.shape)
    anomaly_ref[...] = (local - mean).astype(BF16)
    yt_ref[...] = y_ref[...].T
    gram_ref[...] = jnp.dot(yt_ref[...], y_ref[...], preferred_element_type=F32)
    cover_ref[...] = jnp.dot(yt_ref[...], anomaly_ref[...], preferred_element_type=F32)

    n = index_ref.shape[1]
    hit = iota((half, n), 0) == index_ref[...]
    observed_mean = jnp.sum(jnp.where(hit, to_col(observed_ref[0:1, :]), 0.0), axis=0, keepdims=True)
    innovation = (value_ref[...] - observed_mean).astype(BF16).astype(F32)
    mask = jnp.where(iota((1, n), 1) < n // 2, mask_ref[0:1, 1:2].astype(F32), mask_ref[0:1, 2:3].astype(F32))
    weight = prec_ref[...].astype(BF16).astype(F32) * mask
    own_d = jnp.sum(jnp.where(hit, weight, 0.0), axis=1, keepdims=True)
    own_g = jnp.sum(jnp.where(hit, weight * innovation, 0.0), axis=1, keepdims=True)
    which = iota((8, half), 0)
    row_ref[...] = jnp.where(which == 0, to_row(own_d), to_row(own_g))
    lane = iota((half, 128), 1)
    col_ref[...] = jnp.where(lane == 0, own_d, own_g)


def analyse_kernel(
    even_ref, mask_ref, anomaly_ref, y_ref, yt_ref, mean_ref, gram_ref, cover_ref, row_ref, col_ref,
    pair_ref, cross_ref, out_ref, z, zt, gram, cover, u,
):
    members, cells = anomaly_ref.shape
    half = cells // 2
    quarter = half // 2

    z[:, :half] = y_ref[...]
    z[:, half : half + quarter] = pair_ref[:members, :]
    z[:, half + quarter :] = cross_ref[:members, :]
    zt[:half, :] = yt_ref[...]
    zt[half:, :] = z[:, half:].T
    rim = jnp.dot(zt[half:, :], z[...], preferred_element_type=F32)
    cross = jnp.dot(yt_ref[...], z[:, half:], preferred_element_type=F32)
    gram[:half, :half] = gram_ref[...]
    gram[:half, half:] = cross
    gram[half:, :] = rim
    cover[:half, :] = cover_ref[...]
    cover[half:, :] = jnp.dot(zt[half:, :], anomaly_ref[...], preferred_element_type=F32)

    mean = mean_ref[0:1, :]
    even = even_ref[0, 0] == 1
    left_mask, right_mask = mask_ref[0:1, 0:1].astype(F32), mask_ref[0:1, 3:4].astype(F32)
    pair_tail = pair_ref[members : members + 16, :].astype(F32)
    cross_tail = cross_ref[members : members + 16, :].astype(F32)
    pair_d = pair_tail[1:2, :] * (0.5 * jnp.where(even, right_mask, left_mask))
    cross_d = cross_tail[1:2, :] * (0.5 * jnp.where(even, left_mask, right_mask))
    pair_g = pair_d * pair_tail[0:1, :]
    cross_g = cross_d * cross_tail[0:1, :]
    d_row = jnp.concatenate([row_ref[0:1, :], pair_d, cross_d], axis=1)
    g_row = jnp.concatenate([row_ref[1:2, :], pair_g, cross_g], axis=1)
    d_col = jnp.concatenate([col_ref[:, 0:1], to_col(pair_d), to_col(cross_d)], axis=0)
    g_col = jnp.concatenate([col_ref[:, 1:2], to_col(pair_g), to_col(cross_g)], axis=0)

    k = gram[...]
    m = cover[...]
    inner = (k * d_col * d_row).astype(BF16)
    u[...] = jnp.dot(z[...], inner, preferred_element_type=F32).astype(BF16)
    most = jnp.zeros((1, 1), F32)
    step = 256
    for i in range(members // step):
        squared = jnp.dot(u[i * step : (i + 1) * step, :], zt[...], preferred_element_type=F32)
        total = jnp.sum(jnp.abs(squared), axis=1, keepdims=True)
        most = jnp.maximum(most, jnp.max(total, axis=0, keepdims=True))
    row_bound = jnp.sqrt(most)
    half_width = (row_bound + 1.0) / 2.0
    theta = 1.0 + half_width
    ratio_sigma = theta / half_width
    rho_first = 1.0 / ratio_sigma
    rho_second = 1.0 / (2.0 * ratio_sigma - rho_first)
    resid_one = 1.0 - 1.0 / theta
    step_one = resid_one / theta
    step_cross = -1.0 / (theta * theta)
    second_one = resid_one - step_one
    second_cross = -1.0 / theta - step_cross - (theta - 1.0) / (theta * theta)
    first_rate = rho_second * rho_first
    second_rate = 2.0 * rho_second / half_width
    to_one = 1.0 / theta + step_one + first_rate * step_one + second_rate * second_one
    to_cross = step_cross + first_rate * step_cross + second_rate * second_cross
    to_square = second_rate / (theta * theta)

    dm = m * d_col
    kdm = jnp.dot(k.astype(BF16), dm.astype(BF16), preferred_element_type=F32)
    gain = (0.5 * to_cross * dm + (0.5 * to_square * d_col) * kdm).astype(BF16)
    once_row = d_row * jnp.sum(k * g_col, axis=0, keepdims=True)
    once_col = d_col * jnp.sum(k * g_row, axis=1, keepdims=True)
    twice_col = d_col * jnp.sum(k * once_row, axis=1, keepdims=True)
    force = to_one * g_col + to_cross * once_col + to_square * twice_col
    shift = mean + jnp.sum(force * m, axis=0, keepdims=True) * (members - 1) ** (-0.5)
    keep = 0.5 * (1.0 + to_one)
    for i in range(members // step):
        at = pl.ds(i * step, step)
        out_ref[at, :] = (
            shift
            + keep * anomaly_ref[at, :].astype(F32)
            + jnp.dot(z[at, :], gain, preferred_element_type=F32)
        ).astype(BF16)


def on_device(ensemble, obs_value, obs_prec, obs_row, obs_col, loc_mask):
    members, fields, rows, cols = ensemble.shape
    bands = lax.axis_size("member")
    domains = lax.axis_size("domain")
    total = members * bands
    cells = fields * (rows // bands) * cols
    n = obs_value.shape[1]
    pairs = [(i, i ^ 1) for i in range(domains)]
    crosses = [(i, (i - 1 + 2 * (i % 2)) % domains) for i in range(domains)]
    struct = jax.ShapeDtypeStruct
    even = (1 - lax.axis_index("domain") % 2).astype(jnp.int32).reshape(1, 1)

    edge = struct((8, members // 8 * fields * rows), F32)
    cross_edge = call(edge_kernel, edge, [even, ensemble], specs=[SMEM, VMEM])
    cross_edge = lax.ppermute(cross_edge, "domain", crosses)
    pair_edge, inside = call(
        inside_kernel,
        [edge, struct((fields, members * rows, cols), F32)],
        [even, ensemble],
        specs=[SMEM, VMEM],
        flops=10**9,
    )
    pair_edge = lax.ppermute(pair_edge, "domain", pairs)
    predicted = call(
        forecast_kernel,
        struct((bands, members, cells), BF16),
        [even, inside, ensemble, pair_edge, cross_edge],
        scratch=[pltpu.VMEM((fields, members * (rows + SKEW), cols), F32)],
        specs=[SMEM] + [VMEM] * 4,
    )
    local = lax.all_to_all(predicted, "member", split_axis=0, concat_axis=0, tiled=True).reshape(total, cells)

    index = obs_row * cols + obs_col
    rim = struct((total + 16, n // 2), BF16)
    y, observed, cross_rows = call(
        observe_kernel,
        [struct((total, cells // 2), BF16), struct((8, cells // 2), F32), rim],
        [even, local, index, obs_value, obs_prec],
        specs=[SMEM] + [VMEM] * 4,
    )
    cross_rows = lax.ppermute(cross_rows, "domain", crosses)
    own = call(
        own_kernel,
        [
            rim,
            struct((total, cells), BF16),
            struct((cells // 2, total), BF16),
            struct((8, cells), F32),
            struct((cells // 2, cells // 2), F32),
            struct((cells // 2, cells), F32),
            struct((8, cells // 2), F32),
            struct((cells // 2, 128), F32),
        ],
        [even, loc_mask, local, y, observed, index, obs_value, obs_prec],
        specs=[SMEM] + [VMEM] * 7,
        flops=2 * total * cells * cells * 3 // 4,
    )
    pair_rows, anomalies, yt, mean, gram, cover, row, col = own
    pair_rows = lax.ppermute(pair_rows, "domain", pairs)
    analysis = call(
        analyse_kernel,
        struct((total, cells), BF16),
        [even, loc_mask, anomalies, y, yt, mean, gram, cover, row, col, pair_rows, cross_rows],
        scratch=[
            pltpu.VMEM((total, cells), BF16),
            pltpu.VMEM((cells, total), BF16),
            pltpu.VMEM((cells, cells), F32),
            pltpu.VMEM((cells, cells), F32),
            pltpu.VMEM((total, cells), BF16),
        ],
        specs=[SMEM] + [VMEM] * 11,
        flops=2 * total * total * cells * 2,
    )
    back = lax.all_to_all(
        analysis.reshape(bands, members, cells), "member", split_axis=0, concat_axis=0, tiled=True
    )
    return call(
        restore_kernel,
        struct(ensemble.shape, BF16),
        [back],
        scratch=[pltpu.VMEM((fields, members * (rows + SKEW), cols), F32)],
    )


def solution(mesh):
    in_specs = (
        P("member", None, None, "domain"),
        P("member", "domain"),
        P("member", "domain"),
        P("member", "domain"),
        P("member", "domain"),
        P("member", "domain"),
    )
    out_specs = P("member", None, None, "domain")
    return jax.shard_map(
        on_device, mesh=mesh, in_specs=in_specs, out_specs=out_specs, check_vma=False
    )
```

```python
import jax
import jax.numpy as jnp
from jax import lax
from jax.experimental import pallas as pl
from jax.experimental.pallas import tpu as pltpu
from jax.sharding import PartitionSpec as P

ADVECT = 0.4
DIFFUSE = 0.15
OBS_WIND = 0.5
SKEW = 4
F32 = jnp.float32
BF16 = jnp.bfloat16
VMEM = pl.BlockSpec(memory_space=pltpu.VMEM)
SMEM = pl.BlockSpec(memory_space=pltpu.SMEM)
HBM = pl.BlockSpec(memory_space=pltpu.HBM)
PARAMS = pltpu.CompilerParams(vmem_limit_bytes=40 * 1024 * 1024)


def call(kernel, shapes, args, scratch=(), specs=None, flops=0, out=VMEM):
    nbytes = sum(a.size * a.dtype.itemsize for a in args)
    return pl.pallas_call(
        kernel,
        out_shape=shapes,
        in_specs=specs or [VMEM] * len(args),
        out_specs=jax.tree.map(lambda _: out, shapes),
        scratch_shapes=list(scratch),
        compiler_params=PARAMS,
        cost_estimate=pl.CostEstimate(flops=flops, bytes_accessed=nbytes, transcendentals=0),
    )(*args)


def iota(shape, dim):
    return lax.broadcasted_iota(jnp.int32, shape, dim)


def to_col(row):
    n = row.shape[1]
    return jnp.sum(jnp.where(iota((n, n), 0) == iota((n, n), 1), row, 0.0), axis=1, keepdims=True)


def to_row(col):
    n = col.shape[0]
    return jnp.sum(jnp.where(iota((n, n), 0) == iota((n, n), 1), col, 0.0), axis=0, keepdims=True)


def write_edges(ens_ref, tail, edge_ref):
    rows, cols = ens_ref.shape[2:]
    pick = (iota((8, cols), 1) == jnp.where(tail, cols - 1, 0)).astype(F32).astype(BF16)
    members = ens_ref.shape[0] // 8
    for k in range(8):
        lines = ens_ref[k * members : (k + 1) * members].reshape(-1, cols)
        edges = lax.dot_general(pick, lines, (((1,), (1,)), ((), ())), preferred_element_type=F32)
        edge_ref[k : k + 1, :] = edges[0:1]


def edge_kernel(even_ref, ens_ref, cross_ref):
    write_edges(ens_ref, even_ref[0, 0] == 0, cross_ref)


def inside_kernel(even_ref, ens_ref, pair_ref, new_ref):
    members, _, rows, cols = ens_ref.shape
    write_edges(ens_ref, even_ref[0, 0] == 1, pair_ref)
    lane = iota((rows, cols), 1)
    for m in range(members):
        wind = None
        for f in range(2):
            x = ens_ref[m, f].astype(F32)
            east = jnp.where(lane == cols - 1, 0.0, pltpu.roll(x, cols - 1, 1))
            west = jnp.where(lane == 0, 0.0, pltpu.roll(x, 1, 1))
            north = pltpu.roll(x, rows - 1, 0)
            south = pltpu.roll(x, 1, 0)
            if f == 0:
                wind = x
            laplace = east + west + north + south - 4.0 * x
            new_ref[f, m * rows : (m + 1) * rows, :] = x - ADVECT * 0.5 * wind * (east - west) + DIFFUSE * laplace


def forecast_kernel(even_ref, new_ref, ens_ref, pair_ref, cross_ref, out_ref, store):
    members, _, rows, cols = ens_ref.shape
    group = members // 8
    pitch = store.shape[1] // members
    even = even_ref[0, 0] == 1
    spot = iota((8, cols), 0)
    lane8 = iota((8, cols), 1)
    pick = jnp.where((spot == 0) & (lane8 == 0) | (spot == 1) & (lane8 == cols - 1), 1.0, 0.0).astype(BF16)
    side = jnp.where(iota((rows, cols), 1) == 0, ADVECT * 0.5, -ADVECT * 0.5)

    for k in range(8):
        n = group * 2 * rows
        which = iota((8, n), 0)
        pair, cross = pair_ref[k : k + 1, :], cross_ref[k : k + 1, :]
        west, east = jnp.where(even, cross, pair), jnp.where(even, pair, cross)
        edges = jnp.where(which == 0, west, jnp.where(which == 1, east, 0.0))
        rim = lax.dot_general(
            edges.astype(BF16), pick, (((0,), (0,)), ((), ())), preferred_element_type=F32
        ).reshape(group * 2, rows, cols)
        for i in range(group):
            m = k * group + i
            rate = side * ens_ref[m, 0].astype(F32) + DIFFUSE
            for f in range(2):
                at = slice(m * rows, (m + 1) * rows)
                store[f, m * pitch : m * pitch + rows, :] = new_ref[f, at, :] + rate * rim[i * 2 + f]
    for f in range(2):
        for r in range(rows):
            part = store[f, pl.ds(r, members, stride=pitch), :]
            at = (f * 2 + r % 2) * cols
            out_ref[r // 2, :, at : at + cols] = part.astype(BF16)


def restore_kernel(in_ref, out_ref, store, done, sems):
    members, _, rows, cols = done.shape
    pitch = store.shape[1] // members
    half = members // 2
    copies = []
    for f in range(2):
        for r in range(rows):
            at = (f * 2 + r % 2) * cols
            store[f, pl.ds(r, members, stride=pitch), :] = in_ref[r // 2, :, at : at + cols].astype(F32)
        for p in range(2):
            for m in range(p * half, (p + 1) * half):
                done[m, f] = store[f, m * pitch : m * pitch + rows, :].astype(BF16)
            part = (pl.ds(p * half, half), f)
            copies.append(pltpu.make_async_copy(done.at[part], out_ref.at[part], sems.at[f * 2 + p]))
            copies[-1].start()
    for copy in copies:
        copy.wait()


def write_rows(side, y_ref, mean, row_ref, col_ref, value_ref, prec_ref, ref):
    members, half = y_ref.shape
    n = row_ref.shape[1] // 2
    at = pl.ds(pl.multiple_of(side * n, n), n)
    hit = iota((half, n), 0) == row_ref[:, at] * (half // 2) + col_ref[:, at]
    ref[:members, :] = jnp.dot(y_ref[...], hit.astype(BF16), preferred_element_type=F32).astype(BF16)
    innovation = value_ref[:, at] - jnp.sum(jnp.where(hit, to_col(mean), 0.0), axis=0, keepdims=True)
    which = iota((16, n), 0)
    last = jnp.where(which == 0, innovation, jnp.where(which == 1, prec_ref[:, at], 0.0))
    ref[members:, :] = last.astype(BF16)


def observe_kernel(even_ref, local_ref, row_ref, col_ref, value_ref, prec_ref, y_ref, mean_ref, cross_ref):
    members, cells = local_ref.shape
    half = cells // 2
    equivalent = local_ref[:, half:].astype(F32) + OBS_WIND * local_ref[:, :half].astype(F32)
    mean = jnp.sum(equivalent, axis=0, keepdims=True) * (1.0 / members)
    mean_ref[...] = jnp.broadcast_to(mean, mean_ref.shape)
    y_ref[...] = ((equivalent - mean) * (members - 1) ** (-0.5)).astype(BF16)
    write_rows(1 - even_ref[0, 0], y_ref, mean, row_ref, col_ref, value_ref, prec_ref, cross_ref)


def own_kernel(
    even_ref, mask_ref, local_ref, y_ref, observed_ref, row_ref, col_ref, value_ref, prec_ref,
    pair_ref, anomaly_ref, yt_ref, mean_ref, gram_ref, cover_ref, across_ref, down_ref,
):
    write_rows(even_ref[0, 0], y_ref, observed_ref[0:1, :], row_ref, col_ref, value_ref, prec_ref, pair_ref)
    members, cells = local_ref.shape
    half = cells // 2
    local = local_ref[...].astype(F32)
    mean = jnp.sum(local, axis=0, keepdims=True) * (1.0 / members)
    mean_ref[...] = jnp.broadcast_to(mean, mean_ref.shape)
    anomaly_ref[...] = (local - mean).astype(BF16)
    yt_ref[...] = y_ref[...].T
    gram_ref[...] = jnp.dot(yt_ref[...], y_ref[...], preferred_element_type=F32)
    cover_ref[...] = jnp.dot(yt_ref[...], anomaly_ref[...], preferred_element_type=F32)

    n = row_ref.shape[1]
    hit = iota((half, n), 0) == row_ref[...] * (half // 2) + col_ref[...]
    observed_mean = jnp.sum(jnp.where(hit, to_col(observed_ref[0:1, :]), 0.0), axis=0, keepdims=True)
    innovation = (value_ref[...] - observed_mean).astype(BF16).astype(F32)
    mask = jnp.where(iota((1, n), 1) < n // 2, mask_ref[0:1, 1:2].astype(F32), mask_ref[0:1, 2:3].astype(F32))
    weight = prec_ref[...].astype(BF16).astype(F32) * mask
    own_d = jnp.sum(jnp.where(hit, weight, 0.0), axis=1, keepdims=True)
    own_g = jnp.sum(jnp.where(hit, weight * innovation, 0.0), axis=1, keepdims=True)
    which = iota((8, half), 0)
    across_ref[...] = jnp.where(which == 0, to_row(own_d), to_row(own_g))
    lane = iota((half, 128), 1)
    down_ref[...] = jnp.where(lane == 0, own_d, own_g)


def analyse_kernel(
    even_ref, mask_ref, anomaly_ref, y_ref, yt_ref, mean_ref, gram_ref, cover_ref, row_ref, col_ref,
    pair_ref, cross_ref, out_ref, z, zt, gram, cover, u,
):
    members, cells = anomaly_ref.shape
    half = cells // 2
    quarter = half // 2

    z[:, :half] = y_ref[...]
    z[:, half : half + quarter] = pair_ref[:members, :]
    z[:, half + quarter :] = cross_ref[:members, :]
    zt[:half, :] = yt_ref[...]
    zt[half:, :] = z[:, half:].T
    rim = jnp.dot(zt[half:, :], z[...], preferred_element_type=F32)
    gram[:half, :half] = gram_ref[...]
    gram[:half, half:] = rim[:, :half].T
    gram[half:, :] = rim
    cover[:half, :] = cover_ref[...]
    cover[half:, :] = jnp.dot(zt[half:, :], anomaly_ref[...], preferred_element_type=F32)

    mean = mean_ref[0:1, :]
    even = even_ref[0, 0] == 1
    left_mask, right_mask = mask_ref[0:1, 0:1].astype(F32), mask_ref[0:1, 3:4].astype(F32)
    pair_tail = pair_ref[members : members + 16, :].astype(F32)
    cross_tail = cross_ref[members : members + 16, :].astype(F32)
    pair_d = pair_tail[1:2, :] * (0.5 * jnp.where(even, right_mask, left_mask))
    cross_d = cross_tail[1:2, :] * (0.5 * jnp.where(even, left_mask, right_mask))
    pair_g = pair_d * pair_tail[0:1, :]
    cross_g = cross_d * cross_tail[0:1, :]
    d_row = jnp.concatenate([row_ref[0:1, :], pair_d, cross_d], axis=1)
    g_row = jnp.concatenate([row_ref[1:2, :], pair_g, cross_g], axis=1)
    d_col = jnp.concatenate([col_ref[:, 0:1], to_col(pair_d), to_col(cross_d)], axis=0)
    g_col = jnp.concatenate([col_ref[:, 1:2], to_col(pair_g), to_col(cross_g)], axis=0)

    k = gram[...]
    m = cover[...]
    inner = (k * d_col * d_row).astype(BF16)
    u[...] = jnp.dot(z[...], inner, preferred_element_type=F32).astype(BF16)
    step = 256
    blocks = members // step
    most = jnp.zeros((1, 1), F32)
    mirrored = [jnp.zeros((1, step), F32) for _ in range(blocks)]
    for i in range(blocks):
        total = jnp.zeros((step, 1), F32)
        for j in range(i, blocks):
            squared = jnp.abs(
                jnp.dot(
                    u[i * step : (i + 1) * step, :], zt[:, j * step : (j + 1) * step], preferred_element_type=F32
                )
            )
            total = total + jnp.sum(squared, axis=1, keepdims=True)
            if j > i:
                mirrored[j] = mirrored[j] + jnp.sum(squared, axis=0, keepdims=True)
        sums = to_row(total) + mirrored[i]
        most = jnp.maximum(most, jnp.max(sums, axis=1, keepdims=True))
    row_bound = jnp.sqrt(most)
    half_width = (row_bound + 1.0) / 2.0
    theta = 1.0 + half_width
    ratio_sigma = theta / half_width
    rho_first = 1.0 / ratio_sigma
    rho_second = 1.0 / (2.0 * ratio_sigma - rho_first)
    resid_one = 1.0 - 1.0 / theta
    step_one = resid_one / theta
    step_cross = -1.0 / (theta * theta)
    second_one = resid_one - step_one
    second_cross = -1.0 / theta - step_cross - (theta - 1.0) / (theta * theta)
    first_rate = rho_second * rho_first
    second_rate = 2.0 * rho_second / half_width
    to_one = 1.0 / theta + step_one + first_rate * step_one + second_rate * second_one
    to_cross = step_cross + first_rate * step_cross + second_rate * second_cross
    to_square = second_rate / (theta * theta)

    dm = m * d_col
    kdm = jnp.dot(k.astype(BF16), dm.astype(BF16), preferred_element_type=F32)
    gain = (0.5 * to_cross * dm + (0.5 * to_square * d_col) * kdm).astype(BF16)
    once_row = d_row * jnp.sum(k * g_col, axis=0, keepdims=True)
    once_col = d_col * jnp.sum(k * g_row, axis=1, keepdims=True)
    twice_col = d_col * jnp.sum(k * once_row, axis=1, keepdims=True)
    force = to_one * g_col + to_cross * once_col + to_square * twice_col
    shift = mean + jnp.sum(force * m, axis=0, keepdims=True) * (members - 1) ** (-0.5)
    keep = 0.5 * (1.0 + to_one)
    for i in range(members // step):
        at = pl.ds(i * step, step)
        out_ref[at, :] = (
            shift
            + keep * anomaly_ref[at, :].astype(F32)
            + jnp.dot(z[at, :], gain, preferred_element_type=F32)
        ).astype(BF16)


def on_device(ensemble, obs_value, obs_prec, obs_row, obs_col, loc_mask):
    members, fields, rows, cols = ensemble.shape
    bands = lax.axis_size("member")
    domains = lax.axis_size("domain")
    total = members * bands
    cells = fields * (rows // bands) * cols
    n = obs_value.shape[1]
    pairs = [(i, i ^ 1) for i in range(domains)]
    crosses = [(i, (i - 1 + 2 * (i % 2)) % domains) for i in range(domains)]
    struct = jax.ShapeDtypeStruct
    even = (1 - lax.axis_index("domain") % 2).astype(jnp.int32).reshape(1, 1)

    edge = struct((8, members // 8 * fields * rows), F32)
    cross_edge = call(edge_kernel, edge, [even, ensemble], specs=[SMEM, VMEM])
    cross_edge = lax.ppermute(cross_edge, "domain", crosses)
    pair_edge, inside = call(
        inside_kernel,
        [edge, struct((fields, members * rows, cols), F32)],
        [even, ensemble],
        specs=[SMEM, VMEM],
        flops=10**9,
    )
    pair_edge = lax.ppermute(pair_edge, "domain", pairs)
    predicted = call(
        forecast_kernel,
        struct((bands, members, cells), BF16),
        [even, inside, ensemble, pair_edge, cross_edge],
        scratch=[pltpu.VMEM((fields, members * (rows + SKEW), cols), F32)],
        specs=[SMEM] + [VMEM] * 4,
    )
    local = lax.all_to_all(predicted, "member", split_axis=0, concat_axis=0, tiled=True).reshape(total, cells)

    rim = struct((total + 16, n // 2), BF16)
    y, observed, cross_rows = call(
        observe_kernel,
        [struct((total, cells // 2), BF16), struct((8, cells // 2), F32), rim],
        [even, local, obs_row, obs_col, obs_value, obs_prec],
        specs=[SMEM] + [VMEM] * 5,
    )
    cross_rows = lax.ppermute(cross_rows, "domain", crosses)
    own = call(
        own_kernel,
        [
            rim,
            struct((total, cells), BF16),
            struct((cells // 2, total), BF16),
            struct((8, cells), F32),
            struct((cells // 2, cells // 2), F32),
            struct((cells // 2, cells), F32),
            struct((8, cells // 2), F32),
            struct((cells // 2, 128), F32),
        ],
        [even, loc_mask, local, y, observed, obs_row, obs_col, obs_value, obs_prec],
        specs=[SMEM] + [VMEM] * 8,
        flops=2 * total * cells * cells * 3 // 4,
    )
    pair_rows, anomalies, yt, mean, gram, cover, row, col = own
    pair_rows = lax.ppermute(pair_rows, "domain", pairs)
    analysis = call(
        analyse_kernel,
        struct((total, cells), BF16),
        [even, loc_mask, anomalies, y, yt, mean, gram, cover, row, col, pair_rows, cross_rows],
        scratch=[
            pltpu.VMEM((total, cells), BF16),
            pltpu.VMEM((cells, total), BF16),
            pltpu.VMEM((cells, cells), F32),
            pltpu.VMEM((cells, cells), F32),
            pltpu.VMEM((total, cells), BF16),
        ],
        specs=[SMEM] + [VMEM] * 11,
        flops=2 * total * total * cells * 2,
    )
    back = lax.all_to_all(
        analysis.reshape(bands, members, cells), "member", split_axis=0, concat_axis=0, tiled=True
    )
    return call(
        restore_kernel,
        struct(ensemble.shape, BF16),
        [back],
        scratch=[
            pltpu.VMEM((fields, members * (rows + SKEW), cols), F32),
            pltpu.VMEM(ensemble.shape, BF16),
            pltpu.SemaphoreType.DMA((4,)),
        ],
        out=HBM,
    )


def solution(mesh):
    in_specs = (
        P("member", None, None, "domain"),
        P("member", "domain"),
        P("member", "domain"),
        P("member", "domain"),
        P("member", "domain"),
        P("member", "domain"),
    )
    out_specs = P("member", None, None, "domain")
    return jax.shard_map(
        on_device, mesh=mesh, in_specs=in_specs, out_specs=out_specs, check_vma=False
    )
```

```python
import jax
import jax.numpy as jnp
from jax import lax
from jax.experimental import pallas as pl
from jax.experimental.pallas import tpu as pltpu
from jax.sharding import PartitionSpec as P

ADVECT = 0.4
DIFFUSE = 0.15
OBS_WIND = 0.5
SKEW = 4
F32 = jnp.float32
BF16 = jnp.bfloat16
VMEM = pl.BlockSpec(memory_space=pltpu.VMEM)
SMEM = pl.BlockSpec(memory_space=pltpu.SMEM)
HBM = pl.BlockSpec(memory_space=pltpu.HBM)
PARAMS = pltpu.CompilerParams(vmem_limit_bytes=40 * 1024 * 1024)


def call(kernel, shapes, args, scratch=(), specs=None, flops=0, out=VMEM):
    nbytes = sum(a.size * a.dtype.itemsize for a in args)
    return pl.pallas_call(
        kernel,
        out_shape=shapes,
        in_specs=specs or [VMEM] * len(args),
        out_specs=jax.tree.map(lambda _: out, shapes),
        scratch_shapes=list(scratch),
        compiler_params=PARAMS,
        cost_estimate=pl.CostEstimate(flops=flops, bytes_accessed=nbytes, transcendentals=0),
    )(*args)


def iota(shape, dim):
    return lax.broadcasted_iota(jnp.int32, shape, dim)


def to_col(row):
    n = row.shape[1]
    return jnp.sum(jnp.where(iota((n, n), 0) == iota((n, n), 1), row, 0.0), axis=1, keepdims=True)


def to_row(col):
    n = col.shape[0]
    return jnp.sum(jnp.where(iota((n, n), 0) == iota((n, n), 1), col, 0.0), axis=0, keepdims=True)


def write_edges(ens_ref, tail, edge_ref):
    rows, cols = ens_ref.shape[2:]
    pick = (iota((8, cols), 1) == jnp.where(tail, cols - 1, 0)).astype(F32).astype(BF16)
    members = ens_ref.shape[0] // 8
    for k in range(8):
        lines = ens_ref[k * members : (k + 1) * members].reshape(-1, cols)
        edges = lax.dot_general(pick, lines, (((1,), (1,)), ((), ())), preferred_element_type=F32)
        edge_ref[k : k + 1, :] = edges[0:1]


def edge_kernel(even_ref, ens_ref, pair_ref, cross_ref):
    write_edges(ens_ref, even_ref[0, 0] == 0, cross_ref)
    write_edges(ens_ref, even_ref[0, 0] == 1, pair_ref)


def inside_kernel(ens_ref, new_ref):
    members, _, rows, cols = ens_ref.shape
    lane = iota((rows, cols), 1)
    for m in range(members):
        wind = None
        for f in range(2):
            x = ens_ref[m, f].astype(F32)
            east = jnp.where(lane == cols - 1, 0.0, pltpu.roll(x, cols - 1, 1))
            west = jnp.where(lane == 0, 0.0, pltpu.roll(x, 1, 1))
            north = pltpu.roll(x, rows - 1, 0)
            south = pltpu.roll(x, 1, 0)
            if f == 0:
                wind = x
            laplace = east + west + north + south - 4.0 * x
            new_ref[f, m * rows : (m + 1) * rows, :] = x - ADVECT * 0.5 * wind * (east - west) + DIFFUSE * laplace


def forecast_kernel(even_ref, new_ref, ens_ref, pair_ref, cross_ref, out_ref, store):
    members, _, rows, cols = ens_ref.shape
    group = members // 8
    pitch = store.shape[1] // members
    even = even_ref[0, 0] == 1
    spot = iota((8, cols), 0)
    lane8 = iota((8, cols), 1)
    pick = jnp.where((spot == 0) & (lane8 == 0) | (spot == 1) & (lane8 == cols - 1), 1.0, 0.0).astype(BF16)
    side = jnp.where(iota((rows, cols), 1) == 0, ADVECT * 0.5, -ADVECT * 0.5)

    for k in range(8):
        n = group * 2 * rows
        which = iota((8, n), 0)
        pair, cross = pair_ref[k : k + 1, :], cross_ref[k : k + 1, :]
        west, east = jnp.where(even, cross, pair), jnp.where(even, pair, cross)
        edges = jnp.where(which == 0, west, jnp.where(which == 1, east, 0.0))
        rim = lax.dot_general(
            edges.astype(BF16), pick, (((0,), (0,)), ((), ())), preferred_element_type=F32
        ).reshape(group * 2, rows, cols)
        for i in range(group):
            m = k * group + i
            rate = side * ens_ref[m, 0].astype(F32) + DIFFUSE
            for f in range(2):
                at = slice(m * rows, (m + 1) * rows)
                store[f, m * pitch : m * pitch + rows, :] = new_ref[f, at, :] + rate * rim[i * 2 + f]
    for f in range(2):
        for r in range(rows):
            part = store[f, pl.ds(r, members, stride=pitch), :]
            at = (f * 2 + r % 2) * cols
            out_ref[r // 2, :, at : at + cols] = part.astype(BF16)


def restore_kernel(in_ref, out_ref, store, done, sems):
    members, _, rows, cols = done.shape
    pitch = store.shape[1] // members
    half = members // 2
    copies = []
    for f in range(2):
        for r in range(rows):
            at = (f * 2 + r % 2) * cols
            store[f, pl.ds(r, members, stride=pitch), :] = in_ref[r // 2, :, at : at + cols].astype(F32)
        for p in range(2):
            for m in range(p * half, (p + 1) * half):
                done[m, f] = store[f, m * pitch : m * pitch + rows, :].astype(BF16)
            part = (pl.ds(p * half, half), f)
            copies.append(pltpu.make_async_copy(done.at[part], out_ref.at[part], sems.at[f * 2 + p]))
            copies[-1].start()
    for copy in copies:
        copy.wait()


def write_rows(side, y_ref, mean, row_ref, col_ref, value_ref, prec_ref, ref):
    members, half = y_ref.shape
    n = row_ref.shape[1] // 2
    at = pl.ds(pl.multiple_of(side * n, n), n)
    hit = iota((half, n), 0) == row_ref[:, at] * (half // 2) + col_ref[:, at]
    ref[:members, :] = jnp.dot(y_ref[...], hit.astype(BF16), preferred_element_type=F32).astype(BF16)
    innovation = value_ref[:, at] - jnp.sum(jnp.where(hit, to_col(mean), 0.0), axis=0, keepdims=True)
    which = iota((16, n), 0)
    last = jnp.where(which == 0, innovation, jnp.where(which == 1, prec_ref[:, at], 0.0))
    ref[members:, :] = last.astype(BF16)


def observe_kernel(even_ref, local_ref, row_ref, col_ref, value_ref, prec_ref, y_ref, mean_ref, cross_ref):
    members, cells = local_ref.shape
    half = cells // 2
    equivalent = local_ref[:, half:].astype(F32) + OBS_WIND * local_ref[:, :half].astype(F32)
    mean = jnp.sum(equivalent, axis=0, keepdims=True) * (1.0 / members)
    mean_ref[...] = jnp.broadcast_to(mean, mean_ref.shape)
    y_ref[...] = ((equivalent - mean) * (members - 1) ** (-0.5)).astype(BF16)
    write_rows(1 - even_ref[0, 0], y_ref, mean, row_ref, col_ref, value_ref, prec_ref, cross_ref)


def own_kernel(
    even_ref, mask_ref, local_ref, y_ref, observed_ref, row_ref, col_ref, value_ref, prec_ref,
    pair_ref, anomaly_ref, yt_ref, mean_ref, gram_ref, cover_ref, across_ref, down_ref,
):
    write_rows(even_ref[0, 0], y_ref, observed_ref[0:1, :], row_ref, col_ref, value_ref, prec_ref, pair_ref)
    members, cells = local_ref.shape
    half = cells // 2
    local = local_ref[...].astype(F32)
    mean = jnp.sum(local, axis=0, keepdims=True) * (1.0 / members)
    mean_ref[...] = jnp.broadcast_to(mean, mean_ref.shape)
    anomaly_ref[...] = (local - mean).astype(BF16)
    yt_ref[...] = y_ref[...].T
    gram_ref[...] = jnp.dot(yt_ref[...], y_ref[...], preferred_element_type=F32)
    cover_ref[...] = jnp.dot(yt_ref[...], anomaly_ref[...], preferred_element_type=F32)

    n = row_ref.shape[1]
    hit = iota((half, n), 0) == row_ref[...] * (half // 2) + col_ref[...]
    observed_mean = jnp.sum(jnp.where(hit, to_col(observed_ref[0:1, :]), 0.0), axis=0, keepdims=True)
    innovation = (value_ref[...] - observed_mean).astype(BF16).astype(F32)
    mask = jnp.where(iota((1, n), 1) < n // 2, mask_ref[0:1, 1:2].astype(F32), mask_ref[0:1, 2:3].astype(F32))
    weight = prec_ref[...].astype(BF16).astype(F32) * mask
    own_d = jnp.sum(jnp.where(hit, weight, 0.0), axis=1, keepdims=True)
    own_g = jnp.sum(jnp.where(hit, weight * innovation, 0.0), axis=1, keepdims=True)
    which = iota((8, half), 0)
    across_ref[...] = jnp.where(which == 0, to_row(own_d), to_row(own_g))
    lane = iota((half, 128), 1)
    down_ref[...] = jnp.where(lane == 0, own_d, own_g)


def analyse_kernel(
    even_ref, mask_ref, anomaly_ref, y_ref, yt_ref, mean_ref, gram_ref, cover_ref, row_ref, col_ref,
    pair_ref, cross_ref, out_ref, z, zt, gram, cover, u,
):
    members, cells = anomaly_ref.shape
    half = cells // 2
    quarter = half // 2

    z[:, :half] = y_ref[...]
    z[:, half : half + quarter] = pair_ref[:members, :]
    z[:, half + quarter :] = cross_ref[:members, :]
    zt[:half, :] = yt_ref[...]
    zt[half:, :] = z[:, half:].T
    rim = jnp.dot(zt[half:, :], z[...], preferred_element_type=F32)
    gram[:half, :half] = gram_ref[...]
    gram[:half, half:] = rim[:, :half].T
    gram[half:, :] = rim
    cover[:half, :] = cover_ref[...]
    cover[half:, :] = jnp.dot(zt[half:, :], anomaly_ref[...], preferred_element_type=F32)

    mean = mean_ref[0:1, :]
    even = even_ref[0, 0] == 1
    left_mask, right_mask = mask_ref[0:1, 0:1].astype(F32), mask_ref[0:1, 3:4].astype(F32)
    pair_tail = pair_ref[members : members + 16, :].astype(F32)
    cross_tail = cross_ref[members : members + 16, :].astype(F32)
    pair_d = pair_tail[1:2, :] * (0.5 * jnp.where(even, right_mask, left_mask))
    cross_d = cross_tail[1:2, :] * (0.5 * jnp.where(even, left_mask, right_mask))
    pair_g = pair_d * pair_tail[0:1, :]
    cross_g = cross_d * cross_tail[0:1, :]
    d_row = jnp.concatenate([row_ref[0:1, :], pair_d, cross_d], axis=1)
    g_row = jnp.concatenate([row_ref[1:2, :], pair_g, cross_g], axis=1)
    d_col = jnp.concatenate([col_ref[:, 0:1], to_col(pair_d), to_col(cross_d)], axis=0)
    g_col = jnp.concatenate([col_ref[:, 1:2], to_col(pair_g), to_col(cross_g)], axis=0)

    k = gram[...]
    m = cover[...]
    inner = (k * d_col * d_row).astype(BF16)
    u[...] = jnp.dot(z[...], inner, preferred_element_type=F32).astype(BF16)
    step = 256
    blocks = members // step
    most = jnp.zeros((1, 1), F32)
    mirrored = [jnp.zeros((1, step), F32) for _ in range(blocks)]
    for i in range(blocks):
        total = jnp.zeros((step, 1), F32)
        for j in range(i, blocks):
            squared = jnp.abs(
                jnp.dot(
                    u[i * step : (i + 1) * step, :], zt[:, j * step : (j + 1) * step], preferred_element_type=F32
                )
            )
            total = total + jnp.sum(squared, axis=1, keepdims=True)
            if j > i:
                mirrored[j] = mirrored[j] + jnp.sum(squared, axis=0, keepdims=True)
        sums = to_row(total) + mirrored[i]
        most = jnp.maximum(most, jnp.max(sums, axis=1, keepdims=True))
    row_bound = jnp.sqrt(most)
    half_width = (row_bound + 1.0) / 2.0
    theta = 1.0 + half_width
    ratio_sigma = theta / half_width
    rho_first = 1.0 / ratio_sigma
    rho_second = 1.0 / (2.0 * ratio_sigma - rho_first)
    resid_one = 1.0 - 1.0 / theta
    step_one = resid_one / theta
    step_cross = -1.0 / (theta * theta)
    second_one = resid_one - step_one
    second_cross = -1.0 / theta - step_cross - (theta - 1.0) / (theta * theta)
    first_rate = rho_second * rho_first
    second_rate = 2.0 * rho_second / half_width
    to_one = 1.0 / theta + step_one + first_rate * step_one + second_rate * second_one
    to_cross = step_cross + first_rate * step_cross + second_rate * second_cross
    to_square = second_rate / (theta * theta)

    dm = m * d_col
    kdm = jnp.dot(k.astype(BF16), dm.astype(BF16), preferred_element_type=F32)
    gain = (0.5 * to_cross * dm + (0.5 * to_square * d_col) * kdm).astype(BF16)
    once_row = d_row * jnp.sum(k * g_col, axis=0, keepdims=True)
    once_col = d_col * jnp.sum(k * g_row, axis=1, keepdims=True)
    twice_col = d_col * jnp.sum(k * once_row, axis=1, keepdims=True)
    force = to_one * g_col + to_cross * once_col + to_square * twice_col
    shift = mean + jnp.sum(force * m, axis=0, keepdims=True) * (members - 1) ** (-0.5)
    keep = 0.5 * (1.0 + to_one)
    for i in range(members // step):
        at = pl.ds(i * step, step)
        out_ref[at, :] = (
            shift
            + keep * anomaly_ref[at, :].astype(F32)
            + jnp.dot(z[at, :], gain, preferred_element_type=F32)
        ).astype(BF16)


def on_device(ensemble, obs_value, obs_prec, obs_row, obs_col, loc_mask):
    members, fields, rows, cols = ensemble.shape
    bands = lax.axis_size("member")
    domains = lax.axis_size("domain")
    total = members * bands
    cells = fields * (rows // bands) * cols
    n = obs_value.shape[1]
    pairs = [(i, i ^ 1) for i in range(domains)]
    crosses = [(i, (i - 1 + 2 * (i % 2)) % domains) for i in range(domains)]
    struct = jax.ShapeDtypeStruct
    even = (1 - lax.axis_index("domain") % 2).astype(jnp.int32).reshape(1, 1)

    edge = struct((8, members // 8 * fields * rows), F32)
    pair_edge, cross_edge = call(edge_kernel, [edge, edge], [even, ensemble], specs=[SMEM, VMEM])
    pair_edge = lax.ppermute(pair_edge, "domain", pairs)
    cross_edge = lax.ppermute(cross_edge, "domain", crosses)
    inside = call(inside_kernel, struct((fields, members * rows, cols), F32), [ensemble], flops=10**9)
    predicted = call(
        forecast_kernel,
        struct((bands, members, cells), BF16),
        [even, inside, ensemble, pair_edge, cross_edge],
        scratch=[pltpu.VMEM((fields, members * (rows + SKEW), cols), F32)],
        specs=[SMEM] + [VMEM] * 4,
    )
    local = lax.all_to_all(predicted, "member", split_axis=0, concat_axis=0, tiled=True).reshape(total, cells)

    rim = struct((total + 16, n // 2), BF16)
    y, observed, cross_rows = call(
        observe_kernel,
        [struct((total, cells // 2), BF16), struct((8, cells // 2), F32), rim],
        [even, local, obs_row, obs_col, obs_value, obs_prec],
        specs=[SMEM] + [VMEM] * 5,
    )
    cross_rows = lax.ppermute(cross_rows, "domain", crosses)
    own = call(
        own_kernel,
        [
            rim,
            struct((total, cells), BF16),
            struct((cells // 2, total), BF16),
            struct((8, cells), F32),
            struct((cells // 2, cells // 2), F32),
            struct((cells // 2, cells), F32),
            struct((8, cells // 2), F32),
            struct((cells // 2, 128), F32),
        ],
        [even, loc_mask, local, y, observed, obs_row, obs_col, obs_value, obs_prec],
        specs=[SMEM] + [VMEM] * 8,
        flops=2 * total * cells * cells * 3 // 4,
    )
    pair_rows, anomalies, yt, mean, gram, cover, row, col = own
    pair_rows = lax.ppermute(pair_rows, "domain", pairs)
    analysis = call(
        analyse_kernel,
        struct((total, cells), BF16),
        [even, loc_mask, anomalies, y, yt, mean, gram, cover, row, col, pair_rows, cross_rows],
        scratch=[
            pltpu.VMEM((total, cells), BF16),
            pltpu.VMEM((cells, total), BF16),
            pltpu.VMEM((cells, cells), F32),
            pltpu.VMEM((cells, cells), F32),
            pltpu.VMEM((total, cells), BF16),
        ],
        specs=[SMEM] + [VMEM] * 11,
        flops=2 * total * total * cells * 2,
    )
    back = lax.all_to_all(
        analysis.reshape(bands, members, cells), "member", split_axis=0, concat_axis=0, tiled=True
    )
    return call(
        restore_kernel,
        struct(ensemble.shape, BF16),
        [back],
        scratch=[
            pltpu.VMEM((fields, members * (rows + SKEW), cols), F32),
            pltpu.VMEM(ensemble.shape, BF16),
            pltpu.SemaphoreType.DMA((4,)),
        ],
        out=HBM,
    )


def solution(mesh):
    in_specs = (
        P("member", None, None, "domain"),
        P("member", "domain"),
        P("member", "domain"),
        P("member", "domain"),
        P("member", "domain"),
        P("member", "domain"),
    )
    out_specs = P("member", None, None, "domain")
    return jax.shard_map(
        on_device, mesh=mesh, in_specs=in_specs, out_specs=out_specs, check_vma=False
    )
```

```python
import jax
import jax.numpy as jnp
from jax import lax
from jax.experimental import pallas as pl
from jax.experimental.pallas import tpu as pltpu
from jax.sharding import PartitionSpec as P

ADVECT = 0.4
DIFFUSE = 0.15
OBS_WIND = 0.5
SKEW = 4
F32 = jnp.float32
BF16 = jnp.bfloat16
VMEM = pl.BlockSpec(memory_space=pltpu.VMEM)
SMEM = pl.BlockSpec(memory_space=pltpu.SMEM)
HBM = pl.BlockSpec(memory_space=pltpu.HBM)
PARAMS = pltpu.CompilerParams(vmem_limit_bytes=40 * 1024 * 1024)


def call(kernel, shapes, args, scratch=(), specs=None, flops=0, out=VMEM):
    nbytes = sum(a.size * a.dtype.itemsize for a in args)
    return pl.pallas_call(
        kernel,
        out_shape=shapes,
        in_specs=specs or [VMEM] * len(args),
        out_specs=jax.tree.map(lambda _: out, shapes),
        scratch_shapes=list(scratch),
        compiler_params=PARAMS,
        cost_estimate=pl.CostEstimate(flops=flops, bytes_accessed=nbytes, transcendentals=0),
    )(*args)


def iota(shape, dim):
    return lax.broadcasted_iota(jnp.int32, shape, dim)


def to_col(row):
    n = row.shape[1]
    return jnp.sum(jnp.where(iota((n, n), 0) == iota((n, n), 1), row, 0.0), axis=1, keepdims=True)


def to_row(col):
    n = col.shape[0]
    return jnp.sum(jnp.where(iota((n, n), 0) == iota((n, n), 1), col, 0.0), axis=0, keepdims=True)


def write_edges(ens_ref, tail, edge_ref):
    rows, cols = ens_ref.shape[2:]
    pick = (iota((8, cols), 1) == jnp.where(tail, cols - 1, 0)).astype(F32).astype(BF16)
    members = ens_ref.shape[0] // 8
    for k in range(8):
        lines = ens_ref[k * members : (k + 1) * members].reshape(-1, cols)
        edges = lax.dot_general(pick, lines, (((1,), (1,)), ((), ())), preferred_element_type=F32)
        edge_ref[k : k + 1, :] = edges[0:1]


def edge_kernel(even_ref, ens_ref, pair_ref, cross_ref):
    write_edges(ens_ref, even_ref[0, 0] == 0, cross_ref)
    write_edges(ens_ref, even_ref[0, 0] == 1, pair_ref)


def inside_kernel(ens_ref, new_ref):
    members, _, rows, cols = ens_ref.shape
    lane = iota((rows, cols), 1)
    for m in range(members):
        wind = None
        for f in range(2):
            x = ens_ref[m, f].astype(F32)
            east = jnp.where(lane == cols - 1, 0.0, pltpu.roll(x, cols - 1, 1))
            west = jnp.where(lane == 0, 0.0, pltpu.roll(x, 1, 1))
            north = pltpu.roll(x, rows - 1, 0)
            south = pltpu.roll(x, 1, 0)
            if f == 0:
                wind = x
            laplace = east + west + north + south - 4.0 * x
            new_ref[f, m * rows : (m + 1) * rows, :] = x - ADVECT * 0.5 * wind * (east - west) + DIFFUSE * laplace


def forecast_kernel(even_ref, new_ref, ens_ref, pair_ref, cross_ref, out_ref, store):
    members, _, rows, cols = ens_ref.shape
    group = members // 8
    pitch = store.shape[1] // members
    even = even_ref[0, 0] == 1
    spot = iota((8, cols), 0)
    lane8 = iota((8, cols), 1)
    pick = jnp.where((spot == 0) & (lane8 == 0) | (spot == 1) & (lane8 == cols - 1), 1.0, 0.0).astype(BF16)
    side = jnp.where(iota((rows, cols), 1) == 0, ADVECT * 0.5, -ADVECT * 0.5)

    for k in range(8):
        n = group * 2 * rows
        which = iota((8, n), 0)
        pair, cross = pair_ref[k : k + 1, :], cross_ref[k : k + 1, :]
        west, east = jnp.where(even, cross, pair), jnp.where(even, pair, cross)
        edges = jnp.where(which == 0, west, jnp.where(which == 1, east, 0.0))
        rim = lax.dot_general(
            edges.astype(BF16), pick, (((0,), (0,)), ((), ())), preferred_element_type=F32
        ).reshape(group * 2, rows, cols)
        for i in range(group):
            m = k * group + i
            rate = side * ens_ref[m, 0].astype(F32) + DIFFUSE
            for f in range(2):
                at = slice(m * rows, (m + 1) * rows)
                store[f, m * pitch : m * pitch + rows, :] = new_ref[f, at, :] + rate * rim[i * 2 + f]
    for f in range(2):
        for r in range(rows):
            part = store[f, pl.ds(r, members, stride=pitch), :]
            at = (f * 2 + r % 2) * cols
            out_ref[r // 2, :, at : at + cols] = part.astype(BF16)


def restore_kernel(in_ref, out_ref, store, done, sems):
    members, _, rows, cols = done.shape
    pitch = store.shape[1] // members
    half = members // 2
    copies = []
    for f in range(2):
        for r in range(rows):
            at = (f * 2 + r % 2) * cols
            store[f, pl.ds(r, members, stride=pitch), :] = in_ref[r // 2, :, at : at + cols].astype(F32)
        for p in range(2):
            for m in range(p * half, (p + 1) * half):
                done[m, f] = store[f, m * pitch : m * pitch + rows, :].astype(BF16)
            part = (pl.ds(p * half, half), f)
            copies.append(pltpu.make_async_copy(done.at[part], out_ref.at[part], sems.at[f * 2 + p]))
            copies[-1].start()
    for copy in copies:
        copy.wait()


def write_rows(side, y_ref, mean, row_ref, col_ref, value_ref, prec_ref, ref):
    members, half = y_ref.shape
    n = row_ref.shape[1] // 2
    at = pl.ds(pl.multiple_of(side * n, n), n)
    hit = iota((half, n), 0) == row_ref[:, at] * (half // 2) + col_ref[:, at]
    ref[:members, :] = jnp.dot(y_ref[...], hit.astype(BF16), preferred_element_type=F32).astype(BF16)
    innovation = value_ref[:, at] - jnp.sum(jnp.where(hit, to_col(mean), 0.0), axis=0, keepdims=True)
    which = iota((16, n), 0)
    last = jnp.where(which == 0, innovation, jnp.where(which == 1, prec_ref[:, at], 0.0))
    ref[members:, :] = last.astype(BF16)


def observe_kernel(
    even_ref, local_ref, row_ref, col_ref, value_ref, prec_ref, y_ref, mean_ref, pair_ref, cross_ref
):
    members, cells = local_ref.shape
    half = cells // 2
    equivalent = local_ref[:, half:].astype(F32) + OBS_WIND * local_ref[:, :half].astype(F32)
    mean = jnp.sum(equivalent, axis=0, keepdims=True) * (1.0 / members)
    mean_ref[...] = jnp.broadcast_to(mean, mean_ref.shape)
    y_ref[...] = ((equivalent - mean) * (members - 1) ** (-0.5)).astype(BF16)
    write_rows(even_ref[0, 0], y_ref, mean, row_ref, col_ref, value_ref, prec_ref, pair_ref)
    write_rows(1 - even_ref[0, 0], y_ref, mean, row_ref, col_ref, value_ref, prec_ref, cross_ref)


def own_kernel(
    mask_ref, local_ref, y_ref, observed_ref, row_ref, col_ref, value_ref, prec_ref,
    anomaly_ref, yt_ref, mean_ref, gram_ref, cover_ref, across_ref, down_ref,
):
    members, cells = local_ref.shape
    half = cells // 2
    local = local_ref[...].astype(F32)
    mean = jnp.sum(local, axis=0, keepdims=True) * (1.0 / members)
    mean_ref[...] = jnp.broadcast_to(mean, mean_ref.shape)
    anomaly_ref[...] = (local - mean).astype(BF16)
    yt_ref[...] = y_ref[...].T
    gram_ref[...] = jnp.dot(yt_ref[...], y_ref[...], preferred_element_type=F32)
    cover_ref[...] = jnp.dot(yt_ref[...], anomaly_ref[...], preferred_element_type=F32)

    n = row_ref.shape[1]
    hit = iota((half, n), 0) == row_ref[...] * (half // 2) + col_ref[...]
    observed_mean = jnp.sum(jnp.where(hit, to_col(observed_ref[0:1, :]), 0.0), axis=0, keepdims=True)
    innovation = (value_ref[...] - observed_mean).astype(BF16).astype(F32)
    mask = jnp.where(iota((1, n), 1) < n // 2, mask_ref[0:1, 1:2].astype(F32), mask_ref[0:1, 2:3].astype(F32))
    weight = prec_ref[...].astype(BF16).astype(F32) * mask
    own_d = jnp.sum(jnp.where(hit, weight, 0.0), axis=1, keepdims=True)
    own_g = jnp.sum(jnp.where(hit, weight * innovation, 0.0), axis=1, keepdims=True)
    which = iota((8, half), 0)
    across_ref[...] = jnp.where(which == 0, to_row(own_d), to_row(own_g))
    lane = iota((half, 128), 1)
    down_ref[...] = jnp.where(lane == 0, own_d, own_g)


def analyse_kernel(
    even_ref, mask_ref, anomaly_ref, y_ref, yt_ref, mean_ref, gram_ref, cover_ref, row_ref, col_ref,
    pair_ref, cross_ref, out_ref, z, zt, gram, cover, u,
):
    members, cells = anomaly_ref.shape
    half = cells // 2
    quarter = half // 2

    z[:, :half] = y_ref[...]
    z[:, half : half + quarter] = pair_ref[:members, :]
    z[:, half + quarter :] = cross_ref[:members, :]
    zt[:half, :] = yt_ref[...]
    zt[half:, :] = z[:, half:].T
    rim = jnp.dot(zt[half:, :], z[...], preferred_element_type=F32)
    gram[:half, :half] = gram_ref[...]
    gram[:half, half:] = rim[:, :half].T
    gram[half:, :] = rim
    cover[:half, :] = cover_ref[...]
    cover[half:, :] = jnp.dot(zt[half:, :], anomaly_ref[...], preferred_element_type=F32)

    mean = mean_ref[0:1, :]
    even = even_ref[0, 0] == 1
    left_mask, right_mask = mask_ref[0:1, 0:1].astype(F32), mask_ref[0:1, 3:4].astype(F32)
    pair_tail = pair_ref[members : members + 16, :].astype(F32)
    cross_tail = cross_ref[members : members + 16, :].astype(F32)
    pair_d = pair_tail[1:2, :] * (0.5 * jnp.where(even, right_mask, left_mask))
    cross_d = cross_tail[1:2, :] * (0.5 * jnp.where(even, left_mask, right_mask))
    pair_g = pair_d * pair_tail[0:1, :]
    cross_g = cross_d * cross_tail[0:1, :]
    d_row = jnp.concatenate([row_ref[0:1, :], pair_d, cross_d], axis=1)
    g_row = jnp.concatenate([row_ref[1:2, :], pair_g, cross_g], axis=1)
    d_col = jnp.concatenate([col_ref[:, 0:1], to_col(pair_d), to_col(cross_d)], axis=0)
    g_col = jnp.concatenate([col_ref[:, 1:2], to_col(pair_g), to_col(cross_g)], axis=0)

    k = gram[...]
    m = cover[...]
    inner = (k * d_col * d_row).astype(BF16)
    u[...] = jnp.dot(z[...], inner, preferred_element_type=F32).astype(BF16)
    step = 256
    blocks = members // step
    most = jnp.zeros((1, 1), F32)
    mirrored = [jnp.zeros((1, step), F32) for _ in range(blocks)]
    for i in range(blocks):
        total = jnp.zeros((step, 1), F32)
        for j in range(i, blocks):
            squared = jnp.abs(
                jnp.dot(
                    u[i * step : (i + 1) * step, :], zt[:, j * step : (j + 1) * step], preferred_element_type=F32
                )
            )
            total = total + jnp.sum(squared, axis=1, keepdims=True)
            if j > i:
                mirrored[j] = mirrored[j] + jnp.sum(squared, axis=0, keepdims=True)
        sums = to_row(total) + mirrored[i]
        most = jnp.maximum(most, jnp.max(sums, axis=1, keepdims=True))
    row_bound = jnp.sqrt(most)
    half_width = (row_bound + 1.0) / 2.0
    theta = 1.0 + half_width
    ratio_sigma = theta / half_width
    rho_first = 1.0 / ratio_sigma
    rho_second = 1.0 / (2.0 * ratio_sigma - rho_first)
    resid_one = 1.0 - 1.0 / theta
    step_one = resid_one / theta
    step_cross = -1.0 / (theta * theta)
    second_one = resid_one - step_one
    second_cross = -1.0 / theta - step_cross - (theta - 1.0) / (theta * theta)
    first_rate = rho_second * rho_first
    second_rate = 2.0 * rho_second / half_width
    to_one = 1.0 / theta + step_one + first_rate * step_one + second_rate * second_one
    to_cross = step_cross + first_rate * step_cross + second_rate * second_cross
    to_square = second_rate / (theta * theta)

    dm = m * d_col
    kdm = jnp.dot(k.astype(BF16), dm.astype(BF16), preferred_element_type=F32)
    gain = (0.5 * to_cross * dm + (0.5 * to_square * d_col) * kdm).astype(BF16)
    once_row = d_row * jnp.sum(k * g_col, axis=0, keepdims=True)
    once_col = d_col * jnp.sum(k * g_row, axis=1, keepdims=True)
    twice_col = d_col * jnp.sum(k * once_row, axis=1, keepdims=True)
    force = to_one * g_col + to_cross * once_col + to_square * twice_col
    shift = mean + jnp.sum(force * m, axis=0, keepdims=True) * (members - 1) ** (-0.5)
    keep = 0.5 * (1.0 + to_one)
    for i in range(members // step):
        at = pl.ds(i * step, step)
        out_ref[at, :] = (
            shift
            + keep * anomaly_ref[at, :].astype(F32)
            + jnp.dot(z[at, :], gain, preferred_element_type=F32)
        ).astype(BF16)


def on_device(ensemble, obs_value, obs_prec, obs_row, obs_col, loc_mask):
    members, fields, rows, cols = ensemble.shape
    bands = lax.axis_size("member")
    domains = lax.axis_size("domain")
    total = members * bands
    cells = fields * (rows // bands) * cols
    n = obs_value.shape[1]
    pairs = [(i, i ^ 1) for i in range(domains)]
    crosses = [(i, (i - 1 + 2 * (i % 2)) % domains) for i in range(domains)]
    struct = jax.ShapeDtypeStruct
    even = (1 - lax.axis_index("domain") % 2).astype(jnp.int32).reshape(1, 1)

    edge = struct((8, members // 8 * fields * rows), F32)
    pair_edge, cross_edge = call(edge_kernel, [edge, edge], [even, ensemble], specs=[SMEM, VMEM])
    pair_edge = lax.ppermute(pair_edge, "domain", pairs)
    cross_edge = lax.ppermute(cross_edge, "domain", crosses)
    inside = call(inside_kernel, struct((fields, members * rows, cols), F32), [ensemble], flops=10**9)
    predicted = call(
        forecast_kernel,
        struct((bands, members, cells), BF16),
        [even, inside, ensemble, pair_edge, cross_edge],
        scratch=[pltpu.VMEM((fields, members * (rows + SKEW), cols), F32)],
        specs=[SMEM] + [VMEM] * 4,
    )
    local = lax.all_to_all(predicted, "member", split_axis=0, concat_axis=0, tiled=True).reshape(total, cells)

    rim = struct((total + 16, n // 2), BF16)
    y, observed, pair_rows, cross_rows = call(
        observe_kernel,
        [struct((total, cells // 2), BF16), struct((8, cells // 2), F32), rim, rim],
        [even, local, obs_row, obs_col, obs_value, obs_prec],
        specs=[SMEM] + [VMEM] * 5,
    )
    pair_rows = lax.ppermute(pair_rows, "domain", pairs)
    cross_rows = lax.ppermute(cross_rows, "domain", crosses)
    own = call(
        own_kernel,
        [
            struct((total, cells), BF16),
            struct((cells // 2, total), BF16),
            struct((8, cells), F32),
            struct((cells // 2, cells // 2), F32),
            struct((cells // 2, cells), F32),
            struct((8, cells // 2), F32),
            struct((cells // 2, 128), F32),
        ],
        [loc_mask, local, y, observed, obs_row, obs_col, obs_value, obs_prec],
        flops=2 * total * cells * cells * 3 // 4,
    )
    anomalies, yt, mean, gram, cover, row, col = own
    analysis = call(
        analyse_kernel,
        struct((total, cells), BF16),
        [even, loc_mask, anomalies, y, yt, mean, gram, cover, row, col, pair_rows, cross_rows],
        scratch=[
            pltpu.VMEM((total, cells), BF16),
            pltpu.VMEM((cells, total), BF16),
            pltpu.VMEM((cells, cells), F32),
            pltpu.VMEM((cells, cells), F32),
            pltpu.VMEM((total, cells), BF16),
        ],
        specs=[SMEM] + [VMEM] * 11,
        flops=2 * total * total * cells * 2,
    )
    back = lax.all_to_all(
        analysis.reshape(bands, members, cells), "member", split_axis=0, concat_axis=0, tiled=True
    )
    return call(
        restore_kernel,
        struct(ensemble.shape, BF16),
        [back],
        scratch=[
            pltpu.VMEM((fields, members * (rows + SKEW), cols), F32),
            pltpu.VMEM(ensemble.shape, BF16),
            pltpu.SemaphoreType.DMA((4,)),
        ],
        out=HBM,
    )


def solution(mesh):
    in_specs = (
        P("member", None, None, "domain"),
        P("member", "domain"),
        P("member", "domain"),
        P("member", "domain"),
        P("member", "domain"),
        P("member", "domain"),
    )
    out_specs = P("member", None, None, "domain")
    return jax.shard_map(
        on_device, mesh=mesh, in_specs=in_specs, out_specs=out_specs, check_vma=False
    )
```

```python
import jax
import jax.numpy as jnp
from jax import lax
from jax.experimental import pallas as pl
from jax.experimental.pallas import tpu as pltpu
from jax.sharding import PartitionSpec as P

ADVECT = 0.4
DIFFUSE = 0.15
OBS_WIND = 0.5
SKEW = 4
F32 = jnp.float32
BF16 = jnp.bfloat16
VMEM = pl.BlockSpec(memory_space=pltpu.VMEM)
SMEM = pl.BlockSpec(memory_space=pltpu.SMEM)
HBM = pl.BlockSpec(memory_space=pltpu.HBM)


def call(kernel, shapes, args, scratch=(), specs=None, flops=0, out=VMEM, limit=40):
    nbytes = sum(a.size * a.dtype.itemsize for a in args)
    return pl.pallas_call(
        kernel,
        out_shape=shapes,
        in_specs=specs or [VMEM] * len(args),
        out_specs=jax.tree.map(lambda _: out, shapes),
        scratch_shapes=list(scratch),
        compiler_params=pltpu.CompilerParams(vmem_limit_bytes=limit * 1024 * 1024),
        cost_estimate=pl.CostEstimate(flops=flops, bytes_accessed=nbytes, transcendentals=0),
    )(*args)


def iota(shape, dim):
    return lax.broadcasted_iota(jnp.int32, shape, dim)


def to_col(row):
    n = row.shape[1]
    return jnp.sum(jnp.where(iota((n, n), 0) == iota((n, n), 1), row, 0.0), axis=1, keepdims=True)


def to_row(col):
    n = col.shape[0]
    return jnp.sum(jnp.where(iota((n, n), 0) == iota((n, n), 1), col, 0.0), axis=0, keepdims=True)


def write_edges(ens_ref, tail, edge_ref, k):
    rows, cols = ens_ref.shape[2:]
    pick = (iota((8, cols), 1) == jnp.where(tail, cols - 1, 0)).astype(F32).astype(BF16)
    members = ens_ref.shape[0] // 8
    lines = ens_ref[k * members : (k + 1) * members].reshape(-1, cols)
    edges = lax.dot_general(pick, lines, (((1,), (1,)), ((), ())), preferred_element_type=F32)
    edge_ref[k : k + 1, :] = edges[0:1]


def edge_kernel(even_ref, ens_ref, pair_ref, cross_ref, here, sems):
    n = here.shape[0] // 8
    copies = [
        pltpu.make_async_copy(ens_ref.at[pl.ds(k * n, n)], here.at[pl.ds(k * n, n)], sems.at[k]) for k in range(8)
    ]
    for copy in copies:
        copy.start()
    for k in range(8):
        copies[k].wait()
        write_edges(here, even_ref[0, 0] == 0, cross_ref, k)
        write_edges(here, even_ref[0, 0] == 1, pair_ref, k)


def inside_kernel(ens_ref, new_ref):
    members, _, rows, cols = ens_ref.shape
    lane = iota((rows, cols), 1)
    for m in range(members):
        wind = None
        for f in range(2):
            x = ens_ref[m, f].astype(F32)
            east = jnp.where(lane == cols - 1, 0.0, pltpu.roll(x, cols - 1, 1))
            west = jnp.where(lane == 0, 0.0, pltpu.roll(x, 1, 1))
            north = pltpu.roll(x, rows - 1, 0)
            south = pltpu.roll(x, 1, 0)
            if f == 0:
                wind = x
            laplace = east + west + north + south - 4.0 * x
            new_ref[f, m * rows : (m + 1) * rows, :] = x - ADVECT * 0.5 * wind * (east - west) + DIFFUSE * laplace


def forecast_kernel(even_ref, new_ref, ens_ref, pair_ref, cross_ref, out_ref, store):
    members, _, rows, cols = ens_ref.shape
    group = members // 8
    pitch = store.shape[1] // members
    even = even_ref[0, 0] == 1
    spot = iota((8, cols), 0)
    lane8 = iota((8, cols), 1)
    pick = jnp.where((spot == 0) & (lane8 == 0) | (spot == 1) & (lane8 == cols - 1), 1.0, 0.0).astype(BF16)
    side = jnp.where(iota((rows, cols), 1) == 0, ADVECT * 0.5, -ADVECT * 0.5)

    for k in range(8):
        n = group * 2 * rows
        which = iota((8, n), 0)
        pair, cross = pair_ref[k : k + 1, :], cross_ref[k : k + 1, :]
        west, east = jnp.where(even, cross, pair), jnp.where(even, pair, cross)
        edges = jnp.where(which == 0, west, jnp.where(which == 1, east, 0.0))
        rim = lax.dot_general(
            edges.astype(BF16), pick, (((0,), (0,)), ((), ())), preferred_element_type=F32
        ).reshape(group * 2, rows, cols)
        for i in range(group):
            m = k * group + i
            rate = side * ens_ref[m, 0].astype(F32) + DIFFUSE
            for f in range(2):
                at = slice(m * rows, (m + 1) * rows)
                store[f, m * pitch : m * pitch + rows, :] = new_ref[f, at, :] + rate * rim[i * 2 + f]
    for f in range(2):
        for r in range(rows):
            part = store[f, pl.ds(r, members, stride=pitch), :]
            at = (f * 2 + r % 2) * cols
            out_ref[r // 2, :, at : at + cols] = part.astype(BF16)


def restore_kernel(in_ref, out_ref, store, done, sems):
    members, _, rows, cols = done.shape
    pitch = store.shape[1] // members
    half = members // 2
    copies = []
    for f in range(2):
        for r in range(rows):
            at = (f * 2 + r % 2) * cols
            store[f, pl.ds(r, members, stride=pitch), :] = in_ref[r // 2, :, at : at + cols].astype(F32)
        for p in range(2):
            for m in range(p * half, (p + 1) * half):
                done[m, f] = store[f, m * pitch : m * pitch + rows, :].astype(BF16)
            part = (pl.ds(p * half, half), f)
            copies.append(pltpu.make_async_copy(done.at[part], out_ref.at[part], sems.at[f * 2 + p]))
            copies[-1].start()
    for copy in copies:
        copy.wait()


def write_rows(side, y_ref, mean, row_ref, col_ref, value_ref, prec_ref, ref):
    members, half = y_ref.shape
    n = row_ref.shape[1] // 2
    at = pl.ds(pl.multiple_of(side * n, n), n)
    hit = iota((half, n), 0) == row_ref[:, at] * (half // 2) + col_ref[:, at]
    ref[:members, :] = jnp.dot(y_ref[...], hit.astype(BF16), preferred_element_type=F32).astype(BF16)
    innovation = value_ref[:, at] - jnp.sum(jnp.where(hit, to_col(mean), 0.0), axis=0, keepdims=True)
    which = iota((16, n), 0)
    last = jnp.where(which == 0, innovation, jnp.where(which == 1, prec_ref[:, at], 0.0))
    ref[members:, :] = last.astype(BF16)


def observe_kernel(even_ref, local_ref, row_ref, col_ref, value_ref, prec_ref, y_ref, mean_ref, cross_ref):
    members, cells = local_ref.shape
    half = cells // 2
    equivalent = local_ref[:, half:].astype(F32) + OBS_WIND * local_ref[:, :half].astype(F32)
    mean = jnp.sum(equivalent, axis=0, keepdims=True) * (1.0 / members)
    mean_ref[...] = jnp.broadcast_to(mean, mean_ref.shape)
    y_ref[...] = ((equivalent - mean) * (members - 1) ** (-0.5)).astype(BF16)
    write_rows(1 - even_ref[0, 0], y_ref, mean, row_ref, col_ref, value_ref, prec_ref, cross_ref)


def own_kernel(
    even_ref, mask_ref, local_ref, y_ref, observed_ref, row_ref, col_ref, value_ref, prec_ref,
    pair_ref, anomaly_ref, yt_ref, mean_ref, gram_ref, cover_ref, across_ref, down_ref,
):
    write_rows(even_ref[0, 0], y_ref, observed_ref[0:1, :], row_ref, col_ref, value_ref, prec_ref, pair_ref)
    members, cells = local_ref.shape
    half = cells // 2
    local = local_ref[...].astype(F32)
    mean = jnp.sum(local, axis=0, keepdims=True) * (1.0 / members)
    mean_ref[...] = jnp.broadcast_to(mean, mean_ref.shape)
    anomaly_ref[...] = (local - mean).astype(BF16)
    yt_ref[...] = y_ref[...].T
    gram_ref[...] = jnp.dot(yt_ref[...], y_ref[...], preferred_element_type=F32)
    cover_ref[...] = jnp.dot(yt_ref[...], anomaly_ref[...], preferred_element_type=F32)

    n = row_ref.shape[1]
    hit = iota((half, n), 0) == row_ref[...] * (half // 2) + col_ref[...]
    observed_mean = jnp.sum(jnp.where(hit, to_col(observed_ref[0:1, :]), 0.0), axis=0, keepdims=True)
    innovation = (value_ref[...] - observed_mean).astype(BF16).astype(F32)
    mask = jnp.where(iota((1, n), 1) < n // 2, mask_ref[0:1, 1:2].astype(F32), mask_ref[0:1, 2:3].astype(F32))
    weight = prec_ref[...].astype(BF16).astype(F32) * mask
    own_d = jnp.sum(jnp.where(hit, weight, 0.0), axis=1, keepdims=True)
    own_g = jnp.sum(jnp.where(hit, weight * innovation, 0.0), axis=1, keepdims=True)
    which = iota((8, half), 0)
    across_ref[...] = jnp.where(which == 0, to_row(own_d), to_row(own_g))
    lane = iota((half, 128), 1)
    down_ref[...] = jnp.where(lane == 0, own_d, own_g)


def analyse_kernel(
    even_ref, mask_ref, anomaly_ref, y_ref, yt_ref, mean_ref, gram_ref, cover_ref, row_ref, col_ref,
    pair_ref, cross_ref, out_ref, z, zt, gram, cover, u,
):
    members, cells = anomaly_ref.shape
    half = cells // 2
    quarter = half // 2

    z[:, :half] = y_ref[...]
    z[:, half : half + quarter] = pair_ref[:members, :]
    z[:, half + quarter :] = cross_ref[:members, :]
    zt[:half, :] = yt_ref[...]
    zt[half:, :] = z[:, half:].T
    rim = jnp.dot(zt[half:, :], z[...], preferred_element_type=F32)
    gram[:half, :half] = gram_ref[...]
    gram[:half, half:] = rim[:, :half].T
    gram[half:, :] = rim
    cover[:half, :] = cover_ref[...]
    cover[half:, :] = jnp.dot(zt[half:, :], anomaly_ref[...], preferred_element_type=F32)

    mean = mean_ref[0:1, :]
    even = even_ref[0, 0] == 1
    left_mask, right_mask = mask_ref[0:1, 0:1].astype(F32), mask_ref[0:1, 3:4].astype(F32)
    pair_tail = pair_ref[members : members + 16, :].astype(F32)
    cross_tail = cross_ref[members : members + 16, :].astype(F32)
    pair_d = pair_tail[1:2, :] * (0.5 * jnp.where(even, right_mask, left_mask))
    cross_d = cross_tail[1:2, :] * (0.5 * jnp.where(even, left_mask, right_mask))
    pair_g = pair_d * pair_tail[0:1, :]
    cross_g = cross_d * cross_tail[0:1, :]
    d_row = jnp.concatenate([row_ref[0:1, :], pair_d, cross_d], axis=1)
    g_row = jnp.concatenate([row_ref[1:2, :], pair_g, cross_g], axis=1)
    d_col = jnp.concatenate([col_ref[:, 0:1], to_col(pair_d), to_col(cross_d)], axis=0)
    g_col = jnp.concatenate([col_ref[:, 1:2], to_col(pair_g), to_col(cross_g)], axis=0)

    k = gram[...]
    m = cover[...]
    inner = (k * d_col * d_row).astype(BF16)
    u[...] = jnp.dot(z[...], inner, preferred_element_type=F32).astype(BF16)
    step = 256
    blocks = members // step
    most = jnp.zeros((1, 1), F32)
    mirrored = [jnp.zeros((1, step), F32) for _ in range(blocks)]
    for i in range(blocks):
        total = jnp.zeros((step, 1), F32)
        for j in range(i, blocks):
            squared = jnp.abs(
                jnp.dot(
                    u[i * step : (i + 1) * step, :], zt[:, j * step : (j + 1) * step], preferred_element_type=F32
                )
            )
            total = total + jnp.sum(squared, axis=1, keepdims=True)
            if j > i:
                mirrored[j] = mirrored[j] + jnp.sum(squared, axis=0, keepdims=True)
        sums = to_row(total) + mirrored[i]
        most = jnp.maximum(most, jnp.max(sums, axis=1, keepdims=True))
    row_bound = jnp.sqrt(most)
    half_width = (row_bound + 1.0) / 2.0
    theta = 1.0 + half_width
    ratio_sigma = theta / half_width
    rho_first = 1.0 / ratio_sigma
    rho_second = 1.0 / (2.0 * ratio_sigma - rho_first)
    resid_one = 1.0 - 1.0 / theta
    step_one = resid_one / theta
    step_cross = -1.0 / (theta * theta)
    second_one = resid_one - step_one
    second_cross = -1.0 / theta - step_cross - (theta - 1.0) / (theta * theta)
    first_rate = rho_second * rho_first
    second_rate = 2.0 * rho_second / half_width
    to_one = 1.0 / theta + step_one + first_rate * step_one + second_rate * second_one
    to_cross = step_cross + first_rate * step_cross + second_rate * second_cross
    to_square = second_rate / (theta * theta)

    dm = m * d_col
    kdm = jnp.dot(k.astype(BF16), dm.astype(BF16), preferred_element_type=F32)
    gain = (0.5 * to_cross * dm + (0.5 * to_square * d_col) * kdm).astype(BF16)
    once_row = d_row * jnp.sum(k * g_col, axis=0, keepdims=True)
    once_col = d_col * jnp.sum(k * g_row, axis=1, keepdims=True)
    twice_col = d_col * jnp.sum(k * once_row, axis=1, keepdims=True)
    force = to_one * g_col + to_cross * once_col + to_square * twice_col
    shift = mean + jnp.sum(force * m, axis=0, keepdims=True) * (members - 1) ** (-0.5)
    keep = 0.5 * (1.0 + to_one)
    for i in range(members // step):
        at = pl.ds(i * step, step)
        out_ref[at, :] = (
            shift
            + keep * anomaly_ref[at, :].astype(F32)
            + jnp.dot(z[at, :], gain, preferred_element_type=F32)
        ).astype(BF16)


def on_device(ensemble, obs_value, obs_prec, obs_row, obs_col, loc_mask):
    members, fields, rows, cols = ensemble.shape
    bands = lax.axis_size("member")
    domains = lax.axis_size("domain")
    total = members * bands
    cells = fields * (rows // bands) * cols
    n = obs_value.shape[1]
    pairs = [(i, i ^ 1) for i in range(domains)]
    crosses = [(i, (i - 1 + 2 * (i % 2)) % domains) for i in range(domains)]
    struct = jax.ShapeDtypeStruct
    even = (1 - lax.axis_index("domain") % 2).astype(jnp.int32).reshape(1, 1)

    edge = struct((8, members // 8 * fields * rows), F32)
    pair_edge, cross_edge = call(
        edge_kernel,
        [edge, edge],
        [even, ensemble],
        scratch=[pltpu.VMEM(ensemble.shape, BF16), pltpu.SemaphoreType.DMA((8,))],
        specs=[SMEM, HBM],
        limit=60,
    )
    pair_edge = lax.ppermute(pair_edge, "domain", pairs)
    cross_edge = lax.ppermute(cross_edge, "domain", crosses)
    inside = call(inside_kernel, struct((fields, members * rows, cols), F32), [ensemble], flops=10**9)
    predicted = call(
        forecast_kernel,
        struct((bands, members, cells), BF16),
        [even, inside, ensemble, pair_edge, cross_edge],
        scratch=[pltpu.VMEM((fields, members * (rows + SKEW), cols), F32)],
        specs=[SMEM] + [VMEM] * 4,
    )
    local = lax.all_to_all(predicted, "member", split_axis=0, concat_axis=0, tiled=True).reshape(total, cells)

    rim = struct((total + 16, n // 2), BF16)
    y, observed, cross_rows = call(
        observe_kernel,
        [struct((total, cells // 2), BF16), struct((8, cells // 2), F32), rim],
        [even, local, obs_row, obs_col, obs_value, obs_prec],
        specs=[SMEM] + [VMEM] * 5,
    )
    cross_rows = lax.ppermute(cross_rows, "domain", crosses)
    own = call(
        own_kernel,
        [
            rim,
            struct((total, cells), BF16),
            struct((cells // 2, total), BF16),
            struct((8, cells), F32),
            struct((cells // 2, cells // 2), F32),
            struct((cells // 2, cells), F32),
            struct((8, cells // 2), F32),
            struct((cells // 2, 128), F32),
        ],
        [even, loc_mask, local, y, observed, obs_row, obs_col, obs_value, obs_prec],
        specs=[SMEM] + [VMEM] * 8,
        flops=2 * total * cells * cells * 3 // 4,
    )
    pair_rows, anomalies, yt, mean, gram, cover, row, col = own
    pair_rows = lax.ppermute(pair_rows, "domain", pairs)
    analysis = call(
        analyse_kernel,
        struct((total, cells), BF16),
        [even, loc_mask, anomalies, y, yt, mean, gram, cover, row, col, pair_rows, cross_rows],
        scratch=[
            pltpu.VMEM((total, cells), BF16),
            pltpu.VMEM((cells, total), BF16),
            pltpu.VMEM((cells, cells), F32),
            pltpu.VMEM((cells, cells), F32),
            pltpu.VMEM((total, cells), BF16),
        ],
        specs=[SMEM] + [VMEM] * 11,
        flops=2 * total * total * cells * 2,
    )
    back = lax.all_to_all(
        analysis.reshape(bands, members, cells), "member", split_axis=0, concat_axis=0, tiled=True
    )
    return call(
        restore_kernel,
        struct(ensemble.shape, BF16),
        [back],
        scratch=[
            pltpu.VMEM((fields, members * (rows + SKEW), cols), F32),
            pltpu.VMEM(ensemble.shape, BF16),
            pltpu.SemaphoreType.DMA((4,)),
        ],
        out=HBM,
    )


def solution(mesh):
    in_specs = (
        P("member", None, None, "domain"),
        P("member", "domain"),
        P("member", "domain"),
        P("member", "domain"),
        P("member", "domain"),
        P("member", "domain"),
    )
    out_specs = P("member", None, None, "domain")
    return jax.shard_map(
        on_device, mesh=mesh, in_specs=in_specs, out_specs=out_specs, check_vma=False
    )
```

```python
import jax
import jax.numpy as jnp
from jax import lax
from jax.experimental import pallas as pl
from jax.experimental.pallas import tpu as pltpu
from jax.sharding import PartitionSpec as P

ADVECT = 0.4
DIFFUSE = 0.15
OBS_WIND = 0.5
SKEW = 4
F32 = jnp.float32
BF16 = jnp.bfloat16
VMEM = pl.BlockSpec(memory_space=pltpu.VMEM)
SMEM = pl.BlockSpec(memory_space=pltpu.SMEM)
HBM = pl.BlockSpec(memory_space=pltpu.HBM)
PARAMS = pltpu.CompilerParams(vmem_limit_bytes=40 * 1024 * 1024)


def call(kernel, shapes, args, scratch=(), specs=None, flops=0, out=VMEM):
    nbytes = sum(a.size * a.dtype.itemsize for a in args)
    return pl.pallas_call(
        kernel,
        out_shape=shapes,
        in_specs=specs or [VMEM] * len(args),
        out_specs=jax.tree.map(lambda _: out, shapes),
        scratch_shapes=list(scratch),
        compiler_params=PARAMS,
        cost_estimate=pl.CostEstimate(flops=flops, bytes_accessed=nbytes, transcendentals=0),
    )(*args)


def iota(shape, dim):
    return lax.broadcasted_iota(jnp.int32, shape, dim)


def to_col(row):
    n = row.shape[1]
    return jnp.sum(jnp.where(iota((n, n), 0) == iota((n, n), 1), row, 0.0), axis=1, keepdims=True)


def to_row(col):
    n = col.shape[0]
    return jnp.sum(jnp.where(iota((n, n), 0) == iota((n, n), 1), col, 0.0), axis=0, keepdims=True)


def write_edges(ens_ref, tail, edge_ref):
    rows, cols = ens_ref.shape[2:]
    pick = (iota((8, cols), 1) == jnp.where(tail, cols - 1, 0)).astype(F32).astype(BF16)
    members = ens_ref.shape[0] // 8
    for k in range(8):
        lines = ens_ref[k * members : (k + 1) * members].reshape(-1, cols)
        edges = lax.dot_general(pick, lines, (((1,), (1,)), ((), ())), preferred_element_type=F32)
        edge_ref[k : k + 1, :] = edges[0:1]


def edge_kernel(even_ref, ens_ref, cross_ref):
    write_edges(ens_ref, even_ref[0, 0] == 0, cross_ref)


def inside_kernel(even_ref, ens_ref, pair_ref, new_ref):
    members, _, rows, cols = ens_ref.shape
    write_edges(ens_ref, even_ref[0, 0] == 1, pair_ref)
    lane = iota((rows, cols), 1)
    for m in range(members):
        wind = None
        for f in range(2):
            x = ens_ref[m, f].astype(F32)
            east = jnp.where(lane == cols - 1, 0.0, pltpu.roll(x, cols - 1, 1))
            west = jnp.where(lane == 0, 0.0, pltpu.roll(x, 1, 1))
            north = pltpu.roll(x, rows - 1, 0)
            south = pltpu.roll(x, 1, 0)
            if f == 0:
                wind = x
            laplace = east + west + north + south - 4.0 * x
            new_ref[f, m * rows : (m + 1) * rows, :] = x - ADVECT * 0.5 * wind * (east - west) + DIFFUSE * laplace


def forecast_kernel(even_ref, new_ref, ens_ref, pair_ref, cross_ref, out_ref, store):
    members, _, rows, cols = ens_ref.shape
    group = members // 8
    pitch = store.shape[1] // members
    even = even_ref[0, 0] == 1
    spot = iota((8, cols), 0)
    lane8 = iota((8, cols), 1)
    pick = jnp.where((spot == 0) & (lane8 == 0) | (spot == 1) & (lane8 == cols - 1), 1.0, 0.0).astype(BF16)
    side = jnp.where(iota((rows, cols), 1) == 0, ADVECT * 0.5, -ADVECT * 0.5)

    for k in range(8):
        n = group * 2 * rows
        which = iota((8, n), 0)
        pair, cross = pair_ref[k : k + 1, :], cross_ref[k : k + 1, :]
        west, east = jnp.where(even, cross, pair), jnp.where(even, pair, cross)
        edges = jnp.where(which == 0, west, jnp.where(which == 1, east, 0.0))
        rim = lax.dot_general(
            edges.astype(BF16), pick, (((0,), (0,)), ((), ())), preferred_element_type=F32
        ).reshape(group * 2, rows, cols)
        for i in range(group):
            m = k * group + i
            rate = side * ens_ref[m, 0].astype(F32) + DIFFUSE
            for f in range(2):
                at = slice(m * rows, (m + 1) * rows)
                store[f, m * pitch : m * pitch + rows, :] = new_ref[f, at, :] + rate * rim[i * 2 + f]
    for f in range(2):
        for r in range(rows):
            part = store[f, pl.ds(r, members, stride=pitch), :]
            at = (f * 2 + r % 2) * cols
            out_ref[r // 2, :, at : at + cols] = part.astype(BF16)


def restore_kernel(wind_ref, tracer_ref, out_ref, store, done, sems):
    members, _, rows, cols = done.shape
    pitch = store.shape[1] // members
    half = members // 2
    copies = []
    for f, in_ref in enumerate((wind_ref, tracer_ref)):
        for r in range(rows):
            at = r % 2 * cols
            store[f, pl.ds(r, members, stride=pitch), :] = in_ref[r // 2, :, at : at + cols].astype(F32)
        for p in range(2):
            for m in range(p * half, (p + 1) * half):
                done[m, f] = store[f, m * pitch : m * pitch + rows, :].astype(BF16)
            part = (pl.ds(p * half, half), f)
            copies.append(pltpu.make_async_copy(done.at[part], out_ref.at[part], sems.at[f * 2 + p]))
            copies[-1].start()
    for copy in copies:
        copy.wait()


def write_rows(side, y_ref, mean, row_ref, col_ref, value_ref, prec_ref, ref):
    members, half = y_ref.shape
    n = row_ref.shape[1] // 2
    at = pl.ds(pl.multiple_of(side * n, n), n)
    hit = iota((half, n), 0) == row_ref[:, at] * (half // 2) + col_ref[:, at]
    ref[:members, :] = jnp.dot(y_ref[...], hit.astype(BF16), preferred_element_type=F32).astype(BF16)
    innovation = value_ref[:, at] - jnp.sum(jnp.where(hit, to_col(mean), 0.0), axis=0, keepdims=True)
    which = iota((16, n), 0)
    last = jnp.where(which == 0, innovation, jnp.where(which == 1, prec_ref[:, at], 0.0))
    ref[members:, :] = last.astype(BF16)


def observe_kernel(even_ref, local_ref, row_ref, col_ref, value_ref, prec_ref, y_ref, mean_ref, cross_ref):
    members, cells = local_ref.shape
    half = cells // 2
    equivalent = local_ref[:, half:].astype(F32) + OBS_WIND * local_ref[:, :half].astype(F32)
    mean = jnp.sum(equivalent, axis=0, keepdims=True) * (1.0 / members)
    mean_ref[...] = jnp.broadcast_to(mean, mean_ref.shape)
    y_ref[...] = ((equivalent - mean) * (members - 1) ** (-0.5)).astype(BF16)
    write_rows(1 - even_ref[0, 0], y_ref, mean, row_ref, col_ref, value_ref, prec_ref, cross_ref)


def own_kernel(
    even_ref, mask_ref, local_ref, y_ref, observed_ref, row_ref, col_ref, value_ref, prec_ref,
    pair_ref, anomaly_ref, yt_ref, mean_ref, gram_ref, cover_ref, across_ref, down_ref,
):
    write_rows(even_ref[0, 0], y_ref, observed_ref[0:1, :], row_ref, col_ref, value_ref, prec_ref, pair_ref)
    members, cells = local_ref.shape
    half = cells // 2
    local = local_ref[...].astype(F32)
    mean = jnp.sum(local, axis=0, keepdims=True) * (1.0 / members)
    mean_ref[...] = jnp.broadcast_to(mean, mean_ref.shape)
    anomaly_ref[...] = (local - mean).astype(BF16)
    yt_ref[...] = y_ref[...].T
    gram_ref[...] = jnp.dot(yt_ref[...], y_ref[...], preferred_element_type=F32)
    cover_ref[...] = jnp.dot(yt_ref[...], anomaly_ref[...], preferred_element_type=F32)

    n = row_ref.shape[1]
    hit = iota((half, n), 0) == row_ref[...] * (half // 2) + col_ref[...]
    observed_mean = jnp.sum(jnp.where(hit, to_col(observed_ref[0:1, :]), 0.0), axis=0, keepdims=True)
    innovation = (value_ref[...] - observed_mean).astype(BF16).astype(F32)
    mask = jnp.where(iota((1, n), 1) < n // 2, mask_ref[0:1, 1:2].astype(F32), mask_ref[0:1, 2:3].astype(F32))
    weight = prec_ref[...].astype(BF16).astype(F32) * mask
    own_d = jnp.sum(jnp.where(hit, weight, 0.0), axis=1, keepdims=True)
    own_g = jnp.sum(jnp.where(hit, weight * innovation, 0.0), axis=1, keepdims=True)
    which = iota((8, half), 0)
    across_ref[...] = jnp.where(which == 0, to_row(own_d), to_row(own_g))
    lane = iota((half, 128), 1)
    down_ref[...] = jnp.where(lane == 0, own_d, own_g)


def analyse_kernel(
    even_ref, mask_ref, anomaly_ref, y_ref, yt_ref, mean_ref, gram_ref, cover_ref, row_ref, col_ref,
    pair_ref, cross_ref, wind_ref, tracer_ref, z, zt, gram, cover, u,
):
    members, cells = anomaly_ref.shape
    half = cells // 2
    quarter = half // 2

    z[:, :half] = y_ref[...]
    z[:, half : half + quarter] = pair_ref[:members, :]
    z[:, half + quarter :] = cross_ref[:members, :]
    zt[:half, :] = yt_ref[...]
    zt[half:, :] = z[:, half:].T
    rim = jnp.dot(zt[half:, :], z[...], preferred_element_type=F32)
    gram[:half, :half] = gram_ref[...]
    gram[:half, half:] = rim[:, :half].T
    gram[half:, :] = rim
    cover[:half, :] = cover_ref[...]
    cover[half:, :] = jnp.dot(zt[half:, :], anomaly_ref[...], preferred_element_type=F32)

    mean = mean_ref[0:1, :]
    even = even_ref[0, 0] == 1
    left_mask, right_mask = mask_ref[0:1, 0:1].astype(F32), mask_ref[0:1, 3:4].astype(F32)
    pair_tail = pair_ref[members : members + 16, :].astype(F32)
    cross_tail = cross_ref[members : members + 16, :].astype(F32)
    pair_d = pair_tail[1:2, :] * (0.5 * jnp.where(even, right_mask, left_mask))
    cross_d = cross_tail[1:2, :] * (0.5 * jnp.where(even, left_mask, right_mask))
    pair_g = pair_d * pair_tail[0:1, :]
    cross_g = cross_d * cross_tail[0:1, :]
    d_row = jnp.concatenate([row_ref[0:1, :], pair_d, cross_d], axis=1)
    g_row = jnp.concatenate([row_ref[1:2, :], pair_g, cross_g], axis=1)
    d_col = jnp.concatenate([col_ref[:, 0:1], to_col(pair_d), to_col(cross_d)], axis=0)
    g_col = jnp.concatenate([col_ref[:, 1:2], to_col(pair_g), to_col(cross_g)], axis=0)

    k = gram[...]
    m = cover[...]
    inner = (k * d_col * d_row).astype(BF16)
    u[...] = jnp.dot(z[...], inner, preferred_element_type=F32).astype(BF16)
    step = 256
    blocks = members // step
    most = jnp.zeros((1, 1), F32)
    mirrored = [jnp.zeros((1, step), F32) for _ in range(blocks)]
    for i in range(blocks):
        total = jnp.zeros((step, 1), F32)
        for j in range(i, blocks):
            squared = jnp.abs(
                jnp.dot(
                    u[i * step : (i + 1) * step, :], zt[:, j * step : (j + 1) * step], preferred_element_type=F32
                )
            )
            total = total + jnp.sum(squared, axis=1, keepdims=True)
            if j > i:
                mirrored[j] = mirrored[j] + jnp.sum(squared, axis=0, keepdims=True)
        sums = to_row(total) + mirrored[i]
        most = jnp.maximum(most, jnp.max(sums, axis=1, keepdims=True))
    row_bound = jnp.sqrt(most)
    half_width = (row_bound + 1.0) / 2.0
    theta = 1.0 + half_width
    ratio_sigma = theta / half_width
    rho_first = 1.0 / ratio_sigma
    rho_second = 1.0 / (2.0 * ratio_sigma - rho_first)
    resid_one = 1.0 - 1.0 / theta
    step_one = resid_one / theta
    step_cross = -1.0 / (theta * theta)
    second_one = resid_one - step_one
    second_cross = -1.0 / theta - step_cross - (theta - 1.0) / (theta * theta)
    first_rate = rho_second * rho_first
    second_rate = 2.0 * rho_second / half_width
    to_one = 1.0 / theta + step_one + first_rate * step_one + second_rate * second_one
    to_cross = step_cross + first_rate * step_cross + second_rate * second_cross
    to_square = second_rate / (theta * theta)

    dm = m * d_col
    kdm = jnp.dot(k.astype(BF16), dm.astype(BF16), preferred_element_type=F32)
    gain = (0.5 * to_cross * dm + (0.5 * to_square * d_col) * kdm).astype(BF16)
    once_row = d_row * jnp.sum(k * g_col, axis=0, keepdims=True)
    once_col = d_col * jnp.sum(k * g_row, axis=1, keepdims=True)
    twice_col = d_col * jnp.sum(k * once_row, axis=1, keepdims=True)
    force = to_one * g_col + to_cross * once_col + to_square * twice_col
    shift = mean + jnp.sum(force * m, axis=0, keepdims=True) * (members - 1) ** (-0.5)
    keep = 0.5 * (1.0 + to_one)
    for i in range(members // step):
        at = pl.ds(i * step, step)
        new = (
            shift
            + keep * anomaly_ref[at, :].astype(F32)
            + jnp.dot(z[at, :], gain, preferred_element_type=F32)
        ).astype(BF16)
        wind_ref[at, :] = new[:, :half]
        tracer_ref[at, :] = new[:, half:]


def on_device(ensemble, obs_value, obs_prec, obs_row, obs_col, loc_mask):
    members, fields, rows, cols = ensemble.shape
    bands = lax.axis_size("member")
    domains = lax.axis_size("domain")
    total = members * bands
    cells = fields * (rows // bands) * cols
    n = obs_value.shape[1]
    pairs = [(i, i ^ 1) for i in range(domains)]
    crosses = [(i, (i - 1 + 2 * (i % 2)) % domains) for i in range(domains)]
    struct = jax.ShapeDtypeStruct
    even = (1 - lax.axis_index("domain") % 2).astype(jnp.int32).reshape(1, 1)

    edge = struct((8, members // 8 * fields * rows), F32)
    cross_edge = call(edge_kernel, edge, [even, ensemble], specs=[SMEM, VMEM])
    cross_edge = lax.ppermute(cross_edge, "domain", crosses)
    pair_edge, inside = call(
        inside_kernel,
        [edge, struct((fields, members * rows, cols), F32)],
        [even, ensemble],
        specs=[SMEM, VMEM],
        flops=10**9,
    )
    pair_edge = lax.ppermute(pair_edge, "domain", pairs)
    predicted = call(
        forecast_kernel,
        struct((bands, members, cells), BF16),
        [even, inside, ensemble, pair_edge, cross_edge],
        scratch=[pltpu.VMEM((fields, members * (rows + SKEW), cols), F32)],
        specs=[SMEM] + [VMEM] * 4,
    )
    local = lax.all_to_all(predicted, "member", split_axis=0, concat_axis=0, tiled=True).reshape(total, cells)

    rim = struct((total + 16, n // 2), BF16)
    y, observed, cross_rows = call(
        observe_kernel,
        [struct((total, cells // 2), BF16), struct((8, cells // 2), F32), rim],
        [even, local, obs_row, obs_col, obs_value, obs_prec],
        specs=[SMEM] + [VMEM] * 5,
    )
    cross_rows = lax.ppermute(cross_rows, "domain", crosses)
    own = call(
        own_kernel,
        [
            rim,
            struct((total, cells), BF16),
            struct((cells // 2, total), BF16),
            struct((8, cells), F32),
            struct((cells // 2, cells // 2), F32),
            struct((cells // 2, cells), F32),
            struct((8, cells // 2), F32),
            struct((cells // 2, 128), F32),
        ],
        [even, loc_mask, local, y, observed, obs_row, obs_col, obs_value, obs_prec],
        specs=[SMEM] + [VMEM] * 8,
        flops=2 * total * cells * cells * 3 // 4,
    )
    pair_rows, anomalies, yt, mean, gram, cover, row, col = own
    pair_rows = lax.ppermute(pair_rows, "domain", pairs)
    analysis = call(
        analyse_kernel,
        [struct((total, cells // 2), BF16)] * 2,
        [even, loc_mask, anomalies, y, yt, mean, gram, cover, row, col, pair_rows, cross_rows],
        scratch=[
            pltpu.VMEM((total, cells), BF16),
            pltpu.VMEM((cells, total), BF16),
            pltpu.VMEM((cells, cells), F32),
            pltpu.VMEM((cells, cells), F32),
            pltpu.VMEM((total, cells), BF16),
        ],
        specs=[SMEM] + [VMEM] * 11,
        flops=2 * total * total * cells * 2,
    )
    back = [
        lax.all_to_all(
            field.reshape(bands, members, cells // 2), "member", split_axis=0, concat_axis=0, tiled=True
        )
        for field in analysis
    ]
    return call(
        restore_kernel,
        struct(ensemble.shape, BF16),
        back,
        scratch=[
            pltpu.VMEM((fields, members * (rows + SKEW), cols), F32),
            pltpu.VMEM(ensemble.shape, BF16),
            pltpu.SemaphoreType.DMA((4,)),
        ],
        out=HBM,
    )


def solution(mesh):
    in_specs = (
        P("member", None, None, "domain"),
        P("member", "domain"),
        P("member", "domain"),
        P("member", "domain"),
        P("member", "domain"),
        P("member", "domain"),
    )
    out_specs = P("member", None, None, "domain")
    return jax.shard_map(
        on_device, mesh=mesh, in_specs=in_specs, out_specs=out_specs, check_vma=False
    )
```

```python
import jax
import jax.numpy as jnp
from jax import lax
from jax.experimental import pallas as pl
from jax.experimental.pallas import tpu as pltpu
from jax.sharding import PartitionSpec as P

ADVECT = 0.4
DIFFUSE = 0.15
OBS_WIND = 0.5
SKEW = 4
F32 = jnp.float32
BF16 = jnp.bfloat16
VMEM = pl.BlockSpec(memory_space=pltpu.VMEM)
SMEM = pl.BlockSpec(memory_space=pltpu.SMEM)
HBM = pl.BlockSpec(memory_space=pltpu.HBM)
PARAMS = pltpu.CompilerParams(vmem_limit_bytes=40 * 1024 * 1024)


def call(kernel, shapes, args, scratch=(), specs=None, flops=0, out=VMEM):
    nbytes = sum(a.size * a.dtype.itemsize for a in args)
    return pl.pallas_call(
        kernel,
        out_shape=shapes,
        in_specs=specs or [VMEM] * len(args),
        out_specs=jax.tree.map(lambda _: out, shapes),
        scratch_shapes=list(scratch),
        compiler_params=PARAMS,
        cost_estimate=pl.CostEstimate(flops=flops, bytes_accessed=nbytes, transcendentals=0),
    )(*args)


def iota(shape, dim):
    return lax.broadcasted_iota(jnp.int32, shape, dim)


def to_col(row):
    n = row.shape[1]
    return jnp.sum(jnp.where(iota((n, n), 0) == iota((n, n), 1), row, 0.0), axis=1, keepdims=True)


def to_row(col):
    n = col.shape[0]
    return jnp.sum(jnp.where(iota((n, n), 0) == iota((n, n), 1), col, 0.0), axis=0, keepdims=True)


def write_edges(ens_ref, tail, edge_ref):
    rows, cols = ens_ref.shape[2:]
    pick = (iota((8, cols), 1) == jnp.where(tail, cols - 1, 0)).astype(F32).astype(BF16)
    members = ens_ref.shape[0] // 8
    for k in range(8):
        lines = ens_ref[k * members : (k + 1) * members].reshape(-1, cols)
        edges = lax.dot_general(pick, lines, (((1,), (1,)), ((), ())), preferred_element_type=F32)
        edge_ref[k : k + 1, :] = edges[0:1]


def edge_kernel(even_ref, ens_ref, cross_ref):
    write_edges(ens_ref, even_ref[0, 0] == 0, cross_ref)


def inside_kernel(even_ref, ens_ref, pair_ref, new_ref):
    members, _, rows, cols = ens_ref.shape
    write_edges(ens_ref, even_ref[0, 0] == 1, pair_ref)
    lane = iota((rows, cols), 1)
    for m in range(members):
        wind = None
        for f in range(2):
            x = ens_ref[m, f].astype(F32)
            east = jnp.where(lane == cols - 1, 0.0, pltpu.roll(x, cols - 1, 1))
            west = jnp.where(lane == 0, 0.0, pltpu.roll(x, 1, 1))
            north = pltpu.roll(x, rows - 1, 0)
            south = pltpu.roll(x, 1, 0)
            if f == 0:
                wind = x
            laplace = east + west + north + south - 4.0 * x
            new_ref[f, m * rows : (m + 1) * rows, :] = x - ADVECT * 0.5 * wind * (east - west) + DIFFUSE * laplace


def forecast_kernel(even_ref, new_ref, ens_ref, pair_ref, cross_ref, out_ref, store):
    members, _, rows, cols = ens_ref.shape
    group = members // 8
    pitch = store.shape[1] // members
    even = even_ref[0, 0] == 1
    spot = iota((8, cols), 0)
    lane8 = iota((8, cols), 1)
    pick = jnp.where((spot == 0) & (lane8 == 0) | (spot == 1) & (lane8 == cols - 1), 1.0, 0.0).astype(BF16)
    side = jnp.where(iota((rows, cols), 1) == 0, ADVECT * 0.5, -ADVECT * 0.5)

    for k in range(8):
        n = group * 2 * rows
        which = iota((8, n), 0)
        pair, cross = pair_ref[k : k + 1, :], cross_ref[k : k + 1, :]
        west, east = jnp.where(even, cross, pair), jnp.where(even, pair, cross)
        edges = jnp.where(which == 0, west, jnp.where(which == 1, east, 0.0))
        rim = lax.dot_general(
            edges.astype(BF16), pick, (((0,), (0,)), ((), ())), preferred_element_type=F32
        ).reshape(group * 2, rows, cols)
        for i in range(group):
            m = k * group + i
            rate = side * ens_ref[m, 0].astype(F32) + DIFFUSE
            for f in range(2):
                at = slice(m * rows, (m + 1) * rows)
                store[f, m * pitch : m * pitch + rows, :] = new_ref[f, at, :] + rate * rim[i * 2 + f]
    for f in range(2):
        for r in range(rows):
            part = store[f, pl.ds(r, members, stride=pitch), :]
            at = (f * 2 + r % 2) * cols
            out_ref[r // 2, :, at : at + cols] = part.astype(BF16)


def restore_kernel(in_ref, out_ref, store, done, sems):
    members, _, rows, cols = done.shape
    pitch = store.shape[1] // members
    half = members // 2
    copies = []
    for f in range(2):
        for r in range(rows):
            at = (f * 2 + r % 2) * cols
            store[f, pl.ds(r, members, stride=pitch), :] = in_ref[r // 2, :, at : at + cols].astype(F32)
        for p in range(2):
            for m in range(p * half, (p + 1) * half):
                done[m, f] = store[f, m * pitch : m * pitch + rows, :].astype(BF16)
            part = (pl.ds(p * half, half), f)
            copies.append(pltpu.make_async_copy(done.at[part], out_ref.at[part], sems.at[f * 2 + p]))
            copies[-1].start()
    for copy in copies:
        copy.wait()


def write_rows(side, y_ref, mean, row_ref, col_ref, value_ref, prec_ref, ref):
    members, half = y_ref.shape
    n = row_ref.shape[1] // 2
    at = pl.ds(pl.multiple_of(side * n, n), n)
    hit = iota((half, n), 0) == row_ref[:, at] * (half // 2) + col_ref[:, at]
    ref[:members, :] = jnp.dot(y_ref[...], hit.astype(BF16), preferred_element_type=F32).astype(BF16)
    innovation = value_ref[:, at] - jnp.sum(jnp.where(hit, to_col(mean), 0.0), axis=0, keepdims=True)
    which = iota((16, n), 0)
    last = jnp.where(which == 0, innovation, jnp.where(which == 1, prec_ref[:, at], 0.0))
    ref[members:, :] = last.astype(BF16)


def observe_kernel(even_ref, local_ref, row_ref, col_ref, value_ref, prec_ref, y_ref, mean_ref, cross_ref):
    members, cells = local_ref.shape
    half = cells // 2
    equivalent = local_ref[:, half:].astype(F32) + OBS_WIND * local_ref[:, :half].astype(F32)
    mean = jnp.sum(equivalent, axis=0, keepdims=True) * (1.0 / members)
    mean_ref[...] = jnp.broadcast_to(mean, mean_ref.shape)
    y_ref[...] = ((equivalent - mean) * (members - 1) ** (-0.5)).astype(BF16)
    write_rows(1 - even_ref[0, 0], y_ref, mean, row_ref, col_ref, value_ref, prec_ref, cross_ref)


def pair_kernel(even_ref, y_ref, observed_ref, row_ref, col_ref, value_ref, prec_ref, pair_ref, yt_ref):
    write_rows(even_ref[0, 0], y_ref, observed_ref[0:1, :], row_ref, col_ref, value_ref, prec_ref, pair_ref)
    yt_ref[...] = y_ref[...].T


def own_kernel(
    mask_ref, local_ref, y_ref, yt_ref, observed_ref, row_ref, col_ref, value_ref, prec_ref,
    anomaly_ref, mean_ref, gram_ref, cover_ref, across_ref, down_ref,
):
    members, cells = local_ref.shape
    half = cells // 2
    local = local_ref[...].astype(F32)
    mean = jnp.sum(local, axis=0, keepdims=True) * (1.0 / members)
    mean_ref[...] = jnp.broadcast_to(mean, mean_ref.shape)
    anomaly_ref[...] = (local - mean).astype(BF16)
    gram_ref[...] = jnp.dot(yt_ref[...], y_ref[...], preferred_element_type=F32)
    cover_ref[...] = jnp.dot(yt_ref[...], anomaly_ref[...], preferred_element_type=F32)

    n = row_ref.shape[1]
    hit = iota((half, n), 0) == row_ref[...] * (half // 2) + col_ref[...]
    observed_mean = jnp.sum(jnp.where(hit, to_col(observed_ref[0:1, :]), 0.0), axis=0, keepdims=True)
    innovation = (value_ref[...] - observed_mean).astype(BF16).astype(F32)
    mask = jnp.where(iota((1, n), 1) < n // 2, mask_ref[0:1, 1:2].astype(F32), mask_ref[0:1, 2:3].astype(F32))
    weight = prec_ref[...].astype(BF16).astype(F32) * mask
    own_d = jnp.sum(jnp.where(hit, weight, 0.0), axis=1, keepdims=True)
    own_g = jnp.sum(jnp.where(hit, weight * innovation, 0.0), axis=1, keepdims=True)
    which = iota((8, half), 0)
    across_ref[...] = jnp.where(which == 0, to_row(own_d), to_row(own_g))
    lane = iota((half, 128), 1)
    down_ref[...] = jnp.where(lane == 0, own_d, own_g)


def analyse_kernel(
    even_ref, mask_ref, anomaly_ref, y_ref, yt_ref, mean_ref, gram_ref, cover_ref, row_ref, col_ref,
    pair_ref, cross_ref, out_ref, z, zt, gram, cover, u,
):
    members, cells = anomaly_ref.shape
    half = cells // 2
    quarter = half // 2

    z[:, :half] = y_ref[...]
    z[:, half : half + quarter] = pair_ref[:members, :]
    z[:, half + quarter :] = cross_ref[:members, :]
    zt[:half, :] = yt_ref[...]
    zt[half:, :] = z[:, half:].T
    rim = jnp.dot(zt[half:, :], z[...], preferred_element_type=F32)
    gram[:half, :half] = gram_ref[...]
    gram[:half, half:] = rim[:, :half].T
    gram[half:, :] = rim
    cover[:half, :] = cover_ref[...]
    cover[half:, :] = jnp.dot(zt[half:, :], anomaly_ref[...], preferred_element_type=F32)

    mean = mean_ref[0:1, :]
    even = even_ref[0, 0] == 1
    left_mask, right_mask = mask_ref[0:1, 0:1].astype(F32), mask_ref[0:1, 3:4].astype(F32)
    pair_tail = pair_ref[members : members + 16, :].astype(F32)
    cross_tail = cross_ref[members : members + 16, :].astype(F32)
    pair_d = pair_tail[1:2, :] * (0.5 * jnp.where(even, right_mask, left_mask))
    cross_d = cross_tail[1:2, :] * (0.5 * jnp.where(even, left_mask, right_mask))
    pair_g = pair_d * pair_tail[0:1, :]
    cross_g = cross_d * cross_tail[0:1, :]
    d_row = jnp.concatenate([row_ref[0:1, :], pair_d, cross_d], axis=1)
    g_row = jnp.concatenate([row_ref[1:2, :], pair_g, cross_g], axis=1)
    d_col = jnp.concatenate([col_ref[:, 0:1], to_col(pair_d), to_col(cross_d)], axis=0)
    g_col = jnp.concatenate([col_ref[:, 1:2], to_col(pair_g), to_col(cross_g)], axis=0)

    k = gram[...]
    m = cover[...]
    inner = (k * d_col * d_row).astype(BF16)
    u[...] = jnp.dot(z[...], inner, preferred_element_type=F32).astype(BF16)
    step = 256
    blocks = members // step
    most = jnp.zeros((1, 1), F32)
    mirrored = [jnp.zeros((1, step), F32) for _ in range(blocks)]
    for i in range(blocks):
        total = jnp.zeros((step, 1), F32)
        for j in range(i, blocks):
            squared = jnp.abs(
                jnp.dot(
                    u[i * step : (i + 1) * step, :], zt[:, j * step : (j + 1) * step], preferred_element_type=F32
                )
            )
            total = total + jnp.sum(squared, axis=1, keepdims=True)
            if j > i:
                mirrored[j] = mirrored[j] + jnp.sum(squared, axis=0, keepdims=True)
        sums = to_row(total) + mirrored[i]
        most = jnp.maximum(most, jnp.max(sums, axis=1, keepdims=True))
    row_bound = jnp.sqrt(most)
    half_width = (row_bound + 1.0) / 2.0
    theta = 1.0 + half_width
    ratio_sigma = theta / half_width
    rho_first = 1.0 / ratio_sigma
    rho_second = 1.0 / (2.0 * ratio_sigma - rho_first)
    resid_one = 1.0 - 1.0 / theta
    step_one = resid_one / theta
    step_cross = -1.0 / (theta * theta)
    second_one = resid_one - step_one
    second_cross = -1.0 / theta - step_cross - (theta - 1.0) / (theta * theta)
    first_rate = rho_second * rho_first
    second_rate = 2.0 * rho_second / half_width
    to_one = 1.0 / theta + step_one + first_rate * step_one + second_rate * second_one
    to_cross = step_cross + first_rate * step_cross + second_rate * second_cross
    to_square = second_rate / (theta * theta)

    dm = m * d_col
    kdm = jnp.dot(k.astype(BF16), dm.astype(BF16), preferred_element_type=F32)
    gain = (0.5 * to_cross * dm + (0.5 * to_square * d_col) * kdm).astype(BF16)
    once_row = d_row * jnp.sum(k * g_col, axis=0, keepdims=True)
    once_col = d_col * jnp.sum(k * g_row, axis=1, keepdims=True)
    twice_col = d_col * jnp.sum(k * once_row, axis=1, keepdims=True)
    force = to_one * g_col + to_cross * once_col + to_square * twice_col
    shift = mean + jnp.sum(force * m, axis=0, keepdims=True) * (members - 1) ** (-0.5)
    keep = 0.5 * (1.0 + to_one)
    for i in range(members // step):
        at = pl.ds(i * step, step)
        out_ref[at, :] = (
            shift
            + keep * anomaly_ref[at, :].astype(F32)
            + jnp.dot(z[at, :], gain, preferred_element_type=F32)
        ).astype(BF16)


def on_device(ensemble, obs_value, obs_prec, obs_row, obs_col, loc_mask):
    members, fields, rows, cols = ensemble.shape
    bands = lax.axis_size("member")
    domains = lax.axis_size("domain")
    total = members * bands
    cells = fields * (rows // bands) * cols
    n = obs_value.shape[1]
    pairs = [(i, i ^ 1) for i in range(domains)]
    crosses = [(i, (i - 1 + 2 * (i % 2)) % domains) for i in range(domains)]
    struct = jax.ShapeDtypeStruct
    even = (1 - lax.axis_index("domain") % 2).astype(jnp.int32).reshape(1, 1)

    edge = struct((8, members // 8 * fields * rows), F32)
    cross_edge = call(edge_kernel, edge, [even, ensemble], specs=[SMEM, VMEM])
    cross_edge = lax.ppermute(cross_edge, "domain", crosses)
    pair_edge, inside = call(
        inside_kernel,
        [edge, struct((fields, members * rows, cols), F32)],
        [even, ensemble],
        specs=[SMEM, VMEM],
        flops=10**9,
    )
    pair_edge = lax.ppermute(pair_edge, "domain", pairs)
    predicted = call(
        forecast_kernel,
        struct((bands, members, cells), BF16),
        [even, inside, ensemble, pair_edge, cross_edge],
        scratch=[pltpu.VMEM((fields, members * (rows + SKEW), cols), F32)],
        specs=[SMEM] + [VMEM] * 4,
    )
    local = lax.all_to_all(predicted, "member", split_axis=0, concat_axis=0, tiled=True).reshape(total, cells)

    rim = struct((total + 16, n // 2), BF16)
    y, observed, cross_rows = call(
        observe_kernel,
        [struct((total, cells // 2), BF16), struct((8, cells // 2), F32), rim],
        [even, local, obs_row, obs_col, obs_value, obs_prec],
        specs=[SMEM] + [VMEM] * 5,
    )
    cross_rows = lax.ppermute(cross_rows, "domain", crosses)
    pair_rows, yt = call(
        pair_kernel,
        [rim, struct((cells // 2, total), BF16)],
        [even, y, observed, obs_row, obs_col, obs_value, obs_prec],
        specs=[SMEM] + [VMEM] * 6,
        flops=10**9,
    )
    pair_rows = lax.ppermute(pair_rows, "domain", pairs)
    own = call(
        own_kernel,
        [
            struct((total, cells), BF16),
            struct((8, cells), F32),
            struct((cells // 2, cells // 2), F32),
            struct((cells // 2, cells), F32),
            struct((8, cells // 2), F32),
            struct((cells // 2, 128), F32),
        ],
        [loc_mask, local, y, yt, observed, obs_row, obs_col, obs_value, obs_prec],
        flops=2 * total * cells * cells * 3 // 4,
    )
    anomalies, mean, gram, cover, row, col = own
    analysis = call(
        analyse_kernel,
        struct((total, cells), BF16),
        [even, loc_mask, anomalies, y, yt, mean, gram, cover, row, col, pair_rows, cross_rows],
        scratch=[
            pltpu.VMEM((total, cells), BF16),
            pltpu.VMEM((cells, total), BF16),
            pltpu.VMEM((cells, cells), F32),
            pltpu.VMEM((cells, cells), F32),
            pltpu.VMEM((total, cells), BF16),
        ],
        specs=[SMEM] + [VMEM] * 11,
        flops=2 * total * total * cells * 2,
    )
    back = lax.all_to_all(
        analysis.reshape(bands, members, cells), "member", split_axis=0, concat_axis=0, tiled=True
    )
    return call(
        restore_kernel,
        struct(ensemble.shape, BF16),
        [back],
        scratch=[
            pltpu.VMEM((fields, members * (rows + SKEW), cols), F32),
            pltpu.VMEM(ensemble.shape, BF16),
            pltpu.SemaphoreType.DMA((4,)),
        ],
        out=HBM,
    )


def solution(mesh):
    in_specs = (
        P("member", None, None, "domain"),
        P("member", "domain"),
        P("member", "domain"),
        P("member", "domain"),
        P("member", "domain"),
        P("member", "domain"),
    )
    out_specs = P("member", None, None, "domain")
    return jax.shard_map(
        on_device, mesh=mesh, in_specs=in_specs, out_specs=out_specs, check_vma=False
    )
```
